128 devices in a mesh: pb: 8 (over z_hi, y), kv: 8 (over x, z_lo), ha: 2 (over core).
Axes of the slice: x: 4, y: 4, z: 4 (z_hi: 2, z_lo: 2; z = z_hi * 2 + z_lo), core: 2. Of those that a mesh axis runs over, the one named last changes fastest.
Arguments:
- teacher_q: bfloat16 [8192, 4096], P(('pb', 'kv'), 'ha'), may hold values from -240 to 240
- teacher_k: bfloat16 [8192, 1024], P(('pb', 'kv'), 'ha'), may hold values from -6 to 6
- teacher_v: bfloat16 [8192, 1024], P(('pb', 'kv'), 'ha'), may hold values from -6 to 6
- student_q: bfloat16 [8192, 2048], P(('pb', 'kv'), 'ha'), may hold values from -240 to 240
- student_k: bfloat16 [8192, 512], P(('pb', 'kv'), 'ha'), may hold values from -6 to 6
- student_v: bfloat16 [8192, 512], P(('pb', 'kv'), 'ha'), may hold values from -6 to 6
- doc_ids: int32 [8192], P(('pb', 'kv')), may hold values from 0 to 3, never falling along the last dimension, each value on 1 to 6144 neighbouring positions
- proj_weight: bfloat16 [32, 64, 128], replicated, may hold values from -0.75 to 0.75
Outputs:
- grad_w: float32 [2048, 128], P(('pb', 'kv', 'ha'))
- token_loss: float32 [8192], P(('pb', 'kv', 'ha'))
The draws below stay inside these ranges and needn't reach their ends.
Inputs may be any that keep to these rules, and one draw needn't show every extreme that they name: `doc_ids`: document numbers never fall along the sequence; each document spans 1 to 6144 tokens, and one spans exactly that many.
All inputs are finite; a program needn't handle non-finite values.
Results may differ from the reference program's by a relative error of at most 0.0035.
Values may be sent and summed in bfloat16 or wider, within the bound.
No kernel may reach another device: no remote copies, remote signals or barrier semaphores. Data moves between devices by JAX's collectives and lax.ppermute only.
A program may use at most 128 MiB of HBM per device.

```python
import math
import jax
import jax.numpy as jnp
import numpy as np
from jax import lax

QH = 32
KVH = 8
TD = 128
SD = 64
DOCS = 4
TOKENS = 8192


def paired_draw(key, salt, head_size):
    key = jax.random.fold_in(key, salt)
    key_key, query_key = jax.random.split(key, 2)
    per_group = QH // KVH
    keys_raw = jnp.clip(jax.random.normal(key_key, (TOKENS, KVH, head_size), jnp.float32), -6.0, 6.0)
    queries_raw = jnp.clip(jax.random.normal(query_key, (TOKENS, KVH, per_group, head_size), jnp.float32), -6.0, 6.0)
    keys_final = keys_raw
    queries_final = queries_raw
    queries_final = jnp.clip(queries_final, -240.0, 240.0)
    return (queries_final.reshape(TOKENS, QH * head_size), keys_final.reshape(TOKENS, KVH * head_size))


def draw_teacher_q(key, part):
    return paired_draw(key, 5, TD)[0].astype(jnp.bfloat16)


def draw_teacher_k(key, part):
    return paired_draw(key, 5, TD)[1].astype(jnp.bfloat16)


def draw_student_q(key, part):
    return paired_draw(key, 7, SD)[0].astype(jnp.bfloat16)


def draw_student_k(key, part):
    return paired_draw(key, 7, SD)[1].astype(jnp.bfloat16)


def block_levels(rng, extent, pieces, least, top_value):
    level = 1.0
    for axis_at, parts in pieces:
        draws = jax.random.uniform(jax.random.fold_in(jax.random.fold_in(rng, 6), axis_at), (parts,), jnp.float32, least / len(pieces), top_value / len(pieces))
        level = level * jnp.repeat(jnp.exp(draws), extent[axis_at] // parts).reshape((-1,) + (1,) * (len(extent) - 1 - axis_at))
    return level


def profile(amount, total, reach, lean):
    loads = [(1 << 20) // math.isqrt(grade ** lean) + 1 for grade in range(2, amount + 1)]
    surplus, counts = total - reach - (amount - 1), [1] * (amount - 1)
    while surplus > 0:
        free = [i for i in range(amount - 1) if counts[i] < reach]
        pool, budget = sum([loads[i] for i in free]), surplus
        for i in free:
            extra = min(reach - counts[i], max(1, budget * loads[i] // pool), surplus)
            counts[i] = counts[i] + extra
            surplus = surplus - extra
    return np.array([reach] + counts)


def ragged(stream_key, count, total, limit, skew):
    if count == 2:
        one = jax.random.randint(stream_key, (), max(1, total - limit), min(limit, total - 1) + 1)
        return jnp.stack([one, total - one])
    tallies = jnp.asarray(profile(count, total, limit, skew), jnp.int32)
    pairs = (count - 1) // 2
    source_of, taker = tallies[1:1 + 2 * pairs:2], tallies[2:2 + 2 * pairs:2]
    margin = jnp.minimum(source_of - 1, limit - taker)
    shifted = jax.random.randint(jax.random.fold_in(stream_key, 1), (pairs,), 0, 1 << 20) % (margin + 1)
    tallies = tallies.at[1:1 + 2 * pairs:2].set(source_of - shifted).at[2:2 + 2 * pairs:2].set(taker + shifted)
    return tallies[jax.random.permutation(jax.random.fold_in(stream_key, 2), count)]


def noise(own_key, dims, width, most, cuts=(), held_as=jnp.bfloat16):
    drawn = jax.random.normal(own_key, dims, jnp.float32) * width
    if len(cuts) > 0:
        drawn = block_levels(own_key, dims, cuts, -0.22, 0.18) * drawn
    return jnp.clip(drawn, min=-most, max=most).astype(held_as)


def setup_inputs(seed: int = 0) -> dict:
    key_list = jax.random.split(jax.random.key(seed), 9)
    teacher_q = draw_teacher_q(jax.random.fold_in(key_list[8], 71), 0)
    teacher_k = draw_teacher_k(jax.random.fold_in(key_list[8], 71), 0)
    teacher_v = noise(key_list[2], (TOKENS, KVH * TD), 1.0, 6.0, ((0, 64), (1, 2)))
    student_q = draw_student_q(jax.random.fold_in(key_list[8], 71), 0)
    student_k = draw_student_k(jax.random.fold_in(key_list[8], 71), 0)
    student_v = noise(key_list[5], (TOKENS, KVH * SD), 1.0, 6.0, ((0, 64), (1, 2)))
    doc_ids = jnp.searchsorted(jnp.cumsum(ragged(key_list[6], DOCS, TOKENS, 3 * TOKENS // 4, 1)), jnp.arange(TOKENS), side="right").astype(jnp.int32)
    proj_weight = noise(key_list[7], (QH, SD, TD), SD ** -0.5, 0.75)
    return {"teacher_q": teacher_q, "teacher_k": teacher_k, "teacher_v": teacher_v, "student_q": student_q, "student_k": student_k, "student_v": student_v, "doc_ids": doc_ids, "proj_weight": proj_weight}


NEGATIVE = -1e+30
EPSILON = 1e-06

def model_attention(queries, keys_all, values_all, doc_ids, head_size):
    total = queries.shape[0]
    groups = keys_all.shape[1] // head_size
    per_group = queries.shape[1] // (groups * head_size)
    block = math.gcd(total, 256)
    scale = 1.0 / math.sqrt(head_size)
    keyed = keys_all.reshape(total, groups, head_size).astype(jnp.float32)
    valued = values_all.reshape(total, groups, head_size).astype(jnp.float32)
    positions = jnp.arange(total, dtype=jnp.int32)
    query_blocks = queries.reshape(total // block, block, groups, per_group, head_size)
    position_blocks = positions.reshape(total // block, block)
    doc_blocks = doc_ids.reshape(total // block, block)

    def one_block(item):
        query_block, position_block, doc_block = item
        scores = jnp.einsum('qgpd,kgd->gpqk', query_block.astype(jnp.float32), keyed) * scale
        allowed = (doc_block[:, None] == doc_ids[None, :]) & (positions[None, :] <= position_block[:, None])
        scores = jnp.where(allowed, scores, NEGATIVE)
        largest = lax.optimization_barrier(jnp.max(scores, axis=-1, keepdims=True))
        weights = jnp.where(allowed, jnp.exp(scores - largest), 0.0)
        totals = lax.optimization_barrier(jnp.sum(weights, axis=-1))
        rounded = lax.optimization_barrier(weights.astype(jnp.bfloat16)).astype(jnp.float32)
        mixed = jnp.einsum('gpqk,kgd->gpqd', rounded, valued) / totals[..., None]
        return jnp.transpose(mixed, (2, 0, 1, 3)).reshape(block, groups * per_group * head_size)
    outputs = lax.map(one_block, (query_blocks, position_blocks, doc_blocks))
    return outputs.reshape(total, -1).astype(jnp.bfloat16)

def distill(teacher_out, student_out, proj_weight, total_tokens):
    count = teacher_out.shape[0]
    heads = proj_weight.shape[0]
    teacher_float = teacher_out.astype(jnp.float32)
    target = teacher_float * lax.rsqrt(lax.optimization_barrier(jnp.mean(teacher_float * teacher_float, axis=1, keepdims=True)) + EPSILON)
    student_float = student_out.astype(jnp.float32)
    features = (student_float * lax.rsqrt(lax.optimization_barrier(jnp.mean(student_float * student_float, axis=1, keepdims=True)) + EPSILON)).astype(jnp.bfloat16)
    feature_heads = features.reshape(count, heads, -1).astype(jnp.float32)
    predicted = jnp.einsum('thd,hde->the', feature_heads, proj_weight.astype(jnp.float32), precision=lax.Precision.HIGHEST)
    difference = predicted.reshape(count, -1) - target
    token_loss = lax.optimization_barrier(jnp.mean(difference * difference, axis=1))
    gradient = jnp.einsum('thd,the->hde', feature_heads, difference.reshape(count, heads, -1), precision=lax.Precision.HIGHEST)
    gradient = gradient / math.sqrt(total_tokens)
    return (gradient.reshape(-1, gradient.shape[2]), token_loss)

def reference(teacher_q, teacher_k, teacher_v, student_q, student_k, student_v, doc_ids, proj_weight):
    teacher_out = model_attention(teacher_q, teacher_k, teacher_v, doc_ids, TD)
    student_out = model_attention(student_q, student_k, student_v, doc_ids, SD)
    grad_w, token_loss = distill(teacher_out, student_out, proj_weight, TOKENS)
    return (grad_w, token_loss)
```

```python
import functools
import math

import jax
import jax.numpy as jnp
from jax import lax
from jax.experimental import pallas as pl
from jax.experimental.pallas import tpu as pltpu
from jax.sharding import PartitionSpec as P

TD = 128
SD = 64
PB, KV, HA = 8, 8, 2
ROWS = 128
PAD = 16
BLOCK = ROWS + PAD
TOKENS = PB * KV * ROWS
TILE = 512
ALL = ("pb", "kv", "ha")
NEGATIVE = -1e30
EPSILON = 1e-06
LOG2E = 1.4426950408889634
SCALE_T = LOG2E / math.sqrt(TD)
SCALE_S = LOG2E / math.sqrt(SD)
f32 = jnp.float32
bf16 = jnp.bfloat16
VMEM = pltpu.VMEM


def index(pb, kv, ha):
    return (pb * KV + kv) * HA + ha


def core_of(p):
    return (p // 4 + p) % 2


def permute(x, move):
    pairs = [
        (index(p, k, a), index(*move(p, k, a))) for p in range(PB) for k in range(KV) for a in range(HA)
    ]
    return lax.ppermute(x, ALL, pairs)


def from_x(x, step):
    return permute(x, lambda p, k, a: (p, (((k // 2) - step) % 4) * 2 + k % 2, a))


def from_z(x):
    return permute(x, lambda p, k, a: (p, k ^ 1, a))


def from_core(x):
    return permute(x, lambda p, k, a: (p, k, 1 - a))


def params(mib):
    return pltpu.CompilerParams(vmem_limit_bytes=mib * 1024 * 1024)


def whole(space=None):
    return pl.BlockSpec(memory_space=VMEM if space is None else space)


def pack_kernel(info, tq, tk, tv, sq, sk, sv, doc, *outs):
    q_out, kv_out = outs[:4], outs[4:]
    p = info[0]
    lane = lax.broadcasted_iota(jnp.int32, (ROWS, 128), 1)
    ids = doc[...]
    row = lax.broadcasted_iota(jnp.int32, (PAD, 384), 0)
    counts = jnp.zeros((PAD, 384), f32)
    for d in range(1, 4):
        below = jnp.sum(jnp.where(ids < d, 1.0, 0.0), axis=1, keepdims=True)
        counts = jnp.where(row == d, below, counts)
    for j in range(4):
        i = lax.rem(p + j, 4)
        odd = lax.rem(i, 2) == 1
        at = pl.ds(pl.multiple_of(i * 128, 128), 128)
        pair = pl.ds(pl.multiple_of((i // 2) * 128, 128), 128)
        q_out[j][:, 0:512] = tq[:, pl.ds(pl.multiple_of(i * 512, 512), 512)]
        q_out[j][:, 512:768] = sq[:, pl.ds(pl.multiple_of(i * 256, 256), 256)]
        kv_out[j][0:ROWS, 0:128] = tk[:, at]
        kv_out[j][0:ROWS, 128:256] = tv[:, at]
        keys = sk[:, pair].astype(f32)
        values = sv[:, pair].astype(f32)
        keys = jnp.where(odd, pltpu.roll(keys, 64, 1), keys)
        values = jnp.where(odd, values, pltpu.roll(values, 64, 1))
        kv_out[j][0:ROWS, 256:384] = jnp.where(lane < 64, keys, values).astype(bf16)
        kv_out[j][ROWS:BLOCK, :] = counts.astype(bf16)


def pack(info, tq, tk, tv, sq, sk, sv, doc):
    shapes = [jax.ShapeDtypeStruct((ROWS, 768), bf16)] * 4 + [jax.ShapeDtypeStruct((BLOCK, 384), bf16)] * 4
    out = pl.pallas_call(
        pack_kernel,
        out_shape=shapes,
        in_specs=[whole(pltpu.SMEM)] + [whole()] * 7,
        out_specs=[whole()] * 8,
        compiler_params=params(32),
        name="pack",
    )(info, tq, tk, tv, sq, sk, sv, doc)
    return out[:4], out[4:]


def dot_nt(a, b):
    return lax.dot_general(a, b, (((1,), (1,)), ((), ())), preferred_element_type=f32)


def dot_nn(a, b):
    return lax.dot_general(a, b, (((1,), (0,)), ((), ())), preferred_element_type=f32)


def attend_kernel(layout, count, info, *refs):
    q_refs, parts = refs[:4], refs[4 : 4 + count]
    ot_ref, os_ref, ssq_ref = refs[4 + count : 7 + count]
    (kv, ends, qt, qs, st, ss, pt, ps, mt, ms, lt, ls, at, as_, acct, accs, sem) = refs[7 + count :]
    i, k, b = info[0], info[1], info[2]
    chips = [info[4 + u] for u in range(8)]
    copies = []
    slot_at = 0
    for part, blocks in zip(parts, layout):
        for n, (unit, other, j) in enumerate(blocks):
            core = 1 - b if other else b
            low = lax.rem(i - j + 4, 4)
            outer = jnp.where(lax.rem(low, 2) == core, low, low + 4)
            start = pl.multiple_of(outer * 1024 + chips[unit] * 128, 128)
            copies.append(
                pltpu.make_async_copy(part.at[pl.ds(n * BLOCK, ROWS)], kv.at[pl.ds(start, ROWS)], sem)
            )
            copies.append(
                pltpu.make_async_copy(part.at[pl.ds(n * BLOCK + ROWS, PAD)], ends.at[slot_at], sem)
            )
            slot_at += 1
    for c in copies:
        c.start()
    for c in copies:
        c.wait()
    total = jnp.zeros((PAD, 128), f32)
    for n in range(64):
        total = total + ends[n, :, 0:128].astype(f32)
    starts = [jnp.max(total[d : d + 1, :]).astype(jnp.int32) for d in (1, 2, 3)]

    def doc_start(pos):
        at_ = jnp.where(pos >= starts[0], starts[0], 0)
        at_ = jnp.where(pos >= starts[1], starts[1], at_)
        return jnp.where(pos >= starts[2], starts[2], at_)

    def softmax(s_ref, p_ref, m_ref, l_ref, a_ref, scale):
        for r in range(0, 512, 32):
            sl = slice(r, r + 32)
            s = s_ref[sl, :]
            old = m_ref[sl, :]
            new = jnp.maximum(old, jnp.max(s, axis=1, keepdims=True))
            p = jnp.exp2((s - new[:, :1]) * scale)
            a = jnp.exp2((old - new) * scale)
            part_sum = p[:, :128]
            for c in range(128, TILE, 128):
                part_sum = part_sum + p[:, c : c + 128]
            l_ref[sl, :] = l_ref[sl, :] * a + part_sum
            m_ref[sl, :] = new
            a_ref[sl, :] = a
            p_ref[sl, :] = p.astype(bf16)

    def block(slot, carry):
        outer = jnp.where(lax.rem(slot, 2) == b, slot, slot + 4)
        first = outer * 1024 + k * 128
        ds_first, ds_last = doc_start(first), doc_start(first + 127)
        lo, hi = ds_first // TILE, (first + 127) // TILE
        j = lax.rem(i - slot + 4, 4)
        lane = lax.broadcasted_iota(jnp.int32, (ROWS, 128), 1)
        for r in range(4):

            @pl.when(j == r)
            def _(r=r):
                q = q_refs[r]
                for h in range(4):
                    qt[h * 128 : (h + 1) * 128, :] = q[:, h * 128 : (h + 1) * 128]
                for h in range(2):
                    two = q[:, 512 + h * 128 : 512 + (h + 1) * 128].astype(f32)
                    qs[h * 256 : h * 256 + 128, :] = jnp.where(lane < 64, two, 0.0).astype(bf16)
                    qs[h * 256 + 128 : h * 256 + 256, :] = jnp.where(
                        lane < 64, pltpu.roll(two, 64, 1), 0.0
                    ).astype(bf16)

        for ref in (mt, ms):
            ref[...] = jnp.full((512, 128), NEGATIVE, f32)
        for ref in (lt, ls, at, as_, acct, accs):
            ref[...] = jnp.zeros((512, 128), f32)
        ps[...] = jnp.zeros((512, TILE), bf16)

        def keyed(t, c):
            return kv[pl.ds(pl.multiple_of(t * TILE, TILE), TILE), c * 128 : (c + 1) * 128]

        def mask(s_ref, t):
            @pl.when((t * TILE < ds_last) | ((t + 1) * TILE - 1 > first))
            def _():
                qpos = first + lax.broadcasted_iota(jnp.int32, (ROWS, TILE), 0)
                kpos = t * TILE + lax.broadcasted_iota(jnp.int32, (ROWS, TILE), 1)
                ok = (kpos <= qpos) & (kpos >= doc_start(qpos))
                for h in range(4):
                    sl = slice(h * 128, (h + 1) * 128)
                    s_ref[sl, :] = jnp.where(ok, s_ref[sl, :], NEGATIVE)

        st[...] = dot_nt(qt[...], keyed(lo, 0))
        mask(st, lo)

        def step(t, c):
            before, after = jnp.maximum(t - 1, lo), jnp.minimum(t + 1, hi)
            ss[...] = dot_nt(qs[...], keyed(t, 2))
            accs[...] = accs[...] * as_[...] + dot_nn(ps[...], keyed(before, 2))
            softmax(st, pt, mt, lt, at, SCALE_T)
            mask(ss, t)
            st[...] = dot_nt(qt[...], keyed(after, 0))
            acct[...] = acct[...] * at[...] + dot_nn(pt[...], keyed(t, 1))
            softmax(ss, ps, ms, ls, as_, SCALE_S)
            mask(st, after)
            return c

        lax.fori_loop(lo, hi + 1, step, 0)
        student = accs[...] * as_[...] + dot_nn(ps[...], keyed(hi, 2))
        out_t = (acct[...] / jnp.sum(lt[...], axis=1, keepdims=True)).astype(bf16)
        out_s = (student / jnp.sum(ls[...], axis=1, keepdims=True)).astype(bf16)
        ot_ref[slot] = out_t
        os_ref[slot] = out_s
        for n, out in enumerate((out_t, out_s)):
            x = out.astype(f32)
            x = x * x
            x = x[0:128] + x[128:256] + x[256:384] + x[384:512]
            if n == 1:
                x = jnp.where(lane >= 64, x, 0.0)
            x = jnp.broadcast_to(jnp.sum(x, axis=1, keepdims=True), (ROWS, 128))
            ssq_ref[pl.ds(slot + 4 * n, 1), :] = x.T[0:1, :]
        return carry

    lax.fori_loop(0, 4, block, 0)


def attend(info, queries, parts, layout):
    return pl.pallas_call(
        functools.partial(attend_kernel, layout, len(parts)),
        out_shape=[jax.ShapeDtypeStruct((4, 512, 128), bf16)] * 2 + [jax.ShapeDtypeStruct((8, 128), f32)],
        in_specs=[whole(pltpu.SMEM)] + [whole()] * 4 + [whole(pl.ANY)] * len(parts),
        out_specs=[whole()] * 3,
        scratch_shapes=[
            VMEM((TOKENS, 384), bf16),
            VMEM((64, PAD, 384), bf16),
            VMEM((512, 128), bf16),
            VMEM((512, 128), bf16),
            VMEM((512, TILE), f32),
            VMEM((512, TILE), f32),
            VMEM((512, TILE), bf16),
            VMEM((512, TILE), bf16),
        ]
        + [VMEM((512, 128), f32)] * 8
        + [pltpu.SemaphoreType.DMA],
        compiler_params=params(48),
        name="attend",
    )(info, *queries, *parts)


def distill_kernel(ot_ref, os_ref, sums_ref, w_ref, grad_ref, loss_ref):
    sums = sums_ref[0:8, :]
    for n in range(1, 8):
        sums = sums + sums_ref[8 * n : 8 * n + 8, :]
    norm_t = lax.rsqrt(sums[0:4] / (32 * TD) + EPSILON)
    norm_s = lax.rsqrt(sums[4:8] / (32 * SD) + EPSILON)
    column_t = [jnp.broadcast_to(norm_t[s : s + 1, :], (128, 128)).T for s in range(4)]
    column_s = [jnp.broadcast_to(norm_s[s : s + 1, :], (128, 128)).T for s in range(4)]
    losses = [jnp.zeros((128, 128), f32) for s in range(4)]
    for h in range(4):
        weight = jnp.concatenate([jnp.zeros((64, 128), bf16), w_ref[h]], axis=0)
        features, highs, lows = [], [], []
        for s in range(4):
            rows = slice(h * 128, (h + 1) * 128)
            target = ot_ref[s, rows, :].astype(f32) * column_t[s]
            feature = (os_ref[s, rows, :].astype(f32) * column_s[s]).astype(bf16)
            difference = dot_nn(feature, weight) - target
            losses[s] = losses[s] + difference * difference
            high = difference.astype(bf16)
            features.append(feature)
            highs.append(high)
            lows.append((difference - high.astype(f32)).astype(bf16))
        both = jnp.concatenate([jnp.concatenate(highs, axis=0), jnp.concatenate(lows, axis=0)], axis=1)
        result = lax.dot_general(
            jnp.concatenate(features, axis=0), both, (((0,), (0,)), ((), ())), preferred_element_type=f32
        )
        grad_ref[h * 64 : (h + 1) * 64, :] = (result[64:128, 0:128] + result[64:128, 128:256]) * (
            1.0 / math.sqrt(TOKENS)
        )
    for s in range(4):
        loss = jnp.broadcast_to(jnp.sum(losses[s], axis=1, keepdims=True), (128, 128))
        loss_ref[s : s + 1, :] = loss.T[0:1, :] * (1.0 / (32 * TD))


def distill(out_t, out_s, sums, weight):
    return pl.pallas_call(
        distill_kernel,
        out_shape=[jax.ShapeDtypeStruct((256, 128), f32), jax.ShapeDtypeStruct((4, 128), f32)],
        in_specs=[whole()] * 4,
        out_specs=[whole()] * 2,
        compiler_params=params(32),
        name="distill",
    )(out_t, out_s, sums, weight)


def local(teacher_q, teacher_k, teacher_v, student_q, student_k, student_v, doc_ids, proj_weight):
    p, k, a = lax.axis_index("pb"), lax.axis_index("kv"), lax.axis_index("ha")
    x, z = k // 2, k % 2
    info = jnp.stack([p] + [jnp.int32(0)] * 7).astype(jnp.int32)
    queries, keys = pack(
        info, teacher_q, teacher_k, teacher_v, student_q, student_k, student_v, doc_ids.reshape(1, ROWS)
    )

    def to_group(j):
        return lambda p, k, a: (4 * a + (j + p) % 4, k, core_of(p))

    own = jnp.concatenate([permute(keys[j], to_group(j)) for j in range(4)], axis=0)
    queries = [permute(queries[j], to_group(j)) for j in range(4)]
    half = 2 * BLOCK
    right, left, up = from_x(own, 1), from_x(own, -1), from_z(own)
    b1 = from_x(jnp.concatenate([right[:half], up[:half]], axis=0), 1)
    b2 = from_x(jnp.concatenate([left[half:], up[half:]], axis=0), -1)
    b3 = from_z(jnp.concatenate([right[half:], left[:half]], axis=0))
    c1 = from_x(b1[half : half + BLOCK], 1)
    c2 = from_x(b2[half + BLOCK :], -1)
    c3 = from_z(jnp.concatenate([b1[BLOCK:half], b2[:BLOCK]], axis=0))
    parts = [own, right, left, up, b1, b2, b3, c1, c2, c3]
    layout = [
        [(0, j) for j in range(4)],
        [(1, j) for j in range(4)],
        [(2, j) for j in range(4)],
        [(4, j) for j in range(4)],
        [(3, 0), (3, 1), (5, 0), (5, 1)],
        [(3, 2), (3, 3), (6, 2), (6, 3)],
        [(5, 2), (5, 3), (6, 0), (6, 1)],
        [(7, 0)],
        [(7, 3)],
        [(7, 1), (7, 2)],
    ]
    layout = [[(u, o, j) for u, j in blocks] for o in (False, True) for blocks in layout]
    parts = parts + [from_core(part) for part in parts]
    chips = [
        ((x + dx) % 4) * 2 + (z if same else 1 - z) for same in (True, False) for dx in (0, 1, 3, 2)
    ]
    info = jnp.stack([p % 4, k, a, p] + chips + [jnp.int32(0)] * 4).astype(jnp.int32)
    out_t, out_s, sums = attend(info, queries, parts, layout)
    sums = lax.all_to_all(
        jnp.broadcast_to(sums[None], (PB, 8, 128)).reshape(PB * 8, 128), "pb", split_axis=0, concat_axis=0, tiled=True
    )
    weight = lax.dynamic_slice_in_dim(proj_weight, p * 4, 4, axis=0)
    grad, loss = distill(out_t, out_s, sums, weight)
    grad = lax.all_to_all(grad, ("kv", "ha"), split_axis=0, concat_axis=0, tiled=True)
    grad = jnp.sum(grad.reshape(16, 16, 128), axis=0)
    slots = jnp.concatenate([loss, loss], axis=0)
    mine = ((jnp.arange(PB) // 4 + jnp.arange(PB)) % 2) == a
    slots = jnp.where(mine[:, None], slots, 0.0).reshape(PB * HA, 64)
    slots = lax.all_to_all(slots, ("pb", "ha"), split_axis=0, concat_axis=0, tiled=True)
    return grad, jnp.sum(slots, axis=0)


def solution(mesh):
    in_specs = (
        P(("pb", "kv"), "ha"),
        P(("pb", "kv"), "ha"),
        P(("pb", "kv"), "ha"),
        P(("pb", "kv"), "ha"),
        P(("pb", "kv"), "ha"),
        P(("pb", "kv"), "ha"),
        P(("pb", "kv")),
        P(),
    )
    out_specs = (P(("pb", "kv", "ha"), None), P(("pb", "kv", "ha")))
    return jax.shard_map(local, mesh=mesh, in_specs=in_specs, out_specs=out_specs, check_vma=False)
```

```python
import functools
import math

import jax
import jax.numpy as jnp
from jax import lax
from jax.experimental import pallas as pl
from jax.experimental.pallas import tpu as pltpu
from jax.sharding import PartitionSpec as P

TD = 128
SD = 64
PB, KV, HA = 8, 8, 2
ROWS = 128
PAD = 16
BLOCK = ROWS + PAD
UNIT = 4 * ROWS + PAD
TOKENS = PB * KV * ROWS
TILE = 512
COLS = 512
ALL = ("pb", "kv", "ha")
NEGATIVE = -1e30
EPSILON = 1e-06
LOG2E = 1.4426950408889634
SCALE_T = LOG2E / math.sqrt(TD)
SCALE_S = LOG2E / math.sqrt(SD)
f32 = jnp.float32
bf16 = jnp.bfloat16
VMEM = pltpu.VMEM


def index(pb, kv, ha):
    return (pb * KV + kv) * HA + ha


def core_of(p):
    return (p // 4 + p) % 2


def permute(x, move):
    pairs = [
        (index(p, k, a), index(*move(p, k, a))) for p in range(PB) for k in range(KV) for a in range(HA)
    ]
    return lax.ppermute(x, ALL, pairs)


def from_x(x, step):
    return permute(x, lambda p, k, a: (p, (((k // 2) - step) % 4) * 2 + k % 2, a))


def from_z(x):
    return permute(x, lambda p, k, a: (p, k ^ 1, a))


def from_core(x):
    return permute(x, lambda p, k, a: (p, k, 1 - a))


def to_group(j):
    return lambda p, k, a: (4 * a + (j + p) % 4, k, core_of(p))


def params(mib):
    return pltpu.CompilerParams(vmem_limit_bytes=mib * 1024 * 1024)


def whole(space=None):
    return pl.BlockSpec(memory_space=VMEM if space is None else space)


def bring(pairs, sem):
    copies = [pltpu.make_async_copy(src, dst, sem.at[n]) for n, (src, dst) in enumerate(pairs)]
    for c in copies:
        c.start()
    for c in copies:
        c.wait()


def pack_keys_kernel(tk_, tv_, sk_, sv_, doc_, o0, o1, o2, o3, tk, tv, sk, sv, doc, sem):
    bring([(tk_, tk), (tv_, tv), (sk_, sk), (sv_, sv), (doc_, doc)], sem)
    p = lax.axis_index("pb")
    lane = lax.broadcasted_iota(jnp.int32, (ROWS, 128), 1)
    row = lax.broadcasted_iota(jnp.int32, (PAD, 384), 0)
    ids = doc[...]
    counts = [jnp.sum(jnp.where(ids < d, 1.0, 0.0), axis=1, keepdims=True) for d in (1, 2, 3)]
    for j, out in enumerate((o0, o1, o2, o3)):
        i = lax.rem(p + j, 4)
        odd = lax.rem(i, 2) == 1
        at = pl.ds(pl.multiple_of(i * 128, 128), 128)
        pair = pl.ds(pl.multiple_of((i // 2) * 128, 128), 128)
        out[0:ROWS, 0:128] = tk[:, at]
        out[0:ROWS, 128:256] = tv[:, at].astype(f32).T.astype(bf16)
        keys = sk[:, pair].astype(f32)
        keys = jnp.where(odd, pltpu.roll(keys, 64, 1), keys)
        values = sv[:, pair].astype(f32).T
        values = jnp.where(odd, values[64:128], values[0:64])
        values = jnp.concatenate([pltpu.roll(values, 64, 1), values], axis=0)
        out[0:ROWS, 256:384] = jnp.where(lane < 64, keys, values).astype(bf16)
        pad = jnp.zeros((PAD, 384), f32)
        for d in (1, 2, 3):
            pad = jnp.where(row == 4 * j + d, counts[d - 1], pad)
        out[ROWS:BLOCK, :] = pad.astype(bf16)


def pack_keys(tk, tv, sk, sv, doc):
    return pl.pallas_call(
        pack_keys_kernel,
        out_shape=[jax.ShapeDtypeStruct((BLOCK, 384), bf16)] * 4,
        in_specs=[whole(pl.ANY)] * 5,
        out_specs=[whole()] * 4,
        scratch_shapes=[VMEM(x.shape, x.dtype) for x in (tk, tv, sk, sv, doc)]
        + [pltpu.SemaphoreType.DMA((5,))],
        compiler_params=params(56),
        name="pack_keys",
    )(tk, tv, sk, sv, doc)


def pack_queries_kernel(tq_, sq_, o0, o1, o2, o3, tq, sq, sem):
    bring([(tq_, tq), (sq_, sq)], sem)
    p = lax.axis_index("pb")
    for j, out in enumerate((o0, o1, o2, o3)):
        i = lax.rem(p + j, 4)
        out[:, 0:512] = tq[:, pl.ds(pl.multiple_of(i * 512, 512), 512)]
        out[:, 512:768] = sq[:, pl.ds(pl.multiple_of(i * 256, 256), 256)]


def pack_queries(tq, sq):
    return pl.pallas_call(
        pack_queries_kernel,
        out_shape=[jax.ShapeDtypeStruct((ROWS, 768), bf16)] * 4,
        in_specs=[whole(pl.ANY)] * 2,
        out_specs=[whole()] * 4,
        scratch_shapes=[VMEM(x.shape, x.dtype) for x in (tq, sq)] + [pltpu.SemaphoreType.DMA((2,))],
        compiler_params=params(40),
        name="pack_queries",
    )(tq, sq)


def join_kernel(r0, r1, r2, r3, out):
    pad = jnp.zeros((PAD, 384), f32)
    for j, r in enumerate((r0, r1, r2, r3)):
        out[j * ROWS : (j + 1) * ROWS, :] = r[0:ROWS, :]
        pad = pad + r[ROWS:BLOCK, :].astype(f32)
    out[4 * ROWS : UNIT, :] = pad.astype(bf16)


def join(rounds):
    return pl.pallas_call(
        join_kernel,
        out_shape=jax.ShapeDtypeStruct((UNIT, 384), bf16),
        in_specs=[whole()] * 4,
        out_specs=whole(),
        compiler_params=params(8),
        name="join",
    )(*rounds)


def dot_nt(a, b):
    return lax.dot_general(a, b, (((1,), (1,)), ((), ())), preferred_element_type=f32)


def dot_nn(a, b):
    return lax.dot_general(a, b, (((1,), (0,)), ((), ())), preferred_element_type=f32)


def attend_kernel(*refs):
    q_refs, parts = refs[:4], refs[4:20]
    ot_ref, os_ref, ssq_ref = refs[20:23]
    (kt, vt, ks, vs, qt, qs, st, ss, pt, ps, mt, ms, lt, ls, at, as_, acct, accs, sem) = refs[23:]
    i, k, b = lax.rem(lax.axis_index("pb"), 4), lax.axis_index("kv"), lax.axis_index("ha")
    x, z = k // 2, lax.rem(k, 2)
    pairs = []
    total = jnp.zeros((PAD, 128), f32)
    for n in range(16):
        core = b if n < 8 else 1 - b
        unit = n % 8
        dx = (0, 1, 3, 2)[unit % 4]
        chip = lax.rem(x + dx, 4) * 2 + (z if unit < 4 else 1 - z)
        part = parts[n]
        for c, dst in enumerate((kt, vt, ks)):
            lanes = pl.ds(c * 128, 128)
            for j in range(4):
                pairs.append((part.at[pl.ds(j * ROWS, ROWS), lanes], dst.at[core * 4 + j, chip]))
        total = total + part[4 * ROWS : UNIT, 0:128].astype(f32)
    copies = [pltpu.make_async_copy(src, dst, sem) for src, dst in pairs]
    for c in copies:
        c.start()
    starts = []
    for d in (1, 2, 3):
        row = total[d : d + 1] + total[d + 4 : d + 5] + total[d + 8 : d + 9] + total[d + 12 : d + 13]
        starts.append(jnp.max(row).astype(jnp.int32))
    for c in copies:
        c.wait()
    lane = lax.broadcasted_iota(jnp.int32, (64, 128), 1)

    def values_of(n, carry):
        tile = ks[n // 8, lax.rem(n, 8)].astype(f32)
        vs[n // 8, lax.rem(n, 8)] = jnp.where(lane < 64, pltpu.roll(tile[0:64], 64, 1), tile[64:128]).astype(bf16)
        return carry

    lax.fori_loop(0, 64, values_of, 0, unroll=8)

    def doc_start(pos):
        at_ = jnp.where(pos >= starts[0], starts[0], 0)
        at_ = jnp.where(pos >= starts[1], starts[1], at_)
        return jnp.where(pos >= starts[2], starts[2], at_)

    def softmax(s_ref, p_ref, m_ref, l_ref, a_ref, scale):
        old = m_ref[...]
        top = None
        for r in range(0, TILE, 64):
            s = jnp.max(s_ref[r : r + 64, :].reshape(8, 8, COLS), axis=0)
            top = s if top is None else jnp.maximum(top, s)
        new = jnp.maximum(old, jnp.max(top, axis=0, keepdims=True))
        part = None
        for r in range(0, TILE, 64):
            w = jnp.exp2((s_ref[r : r + 64, :].reshape(8, 8, COLS) - new[None]) * scale)
            s = jnp.sum(w, axis=0)
            part = s if part is None else part + s
            p_ref[r : r + 64, :] = w.reshape(64, COLS).astype(bf16)
        a = jnp.exp2((old - new) * scale)
        l_ref[...] = l_ref[...] * a + part
        m_ref[...] = new
        a_ref[...] = a

    def rescale(acc, a):
        n = acc.shape[0] // 8
        return (acc.reshape(n, 8, COLS) * a[None]).reshape(n * 8, COLS)

    def block(slot, carry):
        outer = jnp.where(lax.rem(slot, 2) == b, slot, slot + 4)
        first = outer * 1024 + k * 128
        ds_first, ds_last = doc_start(first), doc_start(first + 127)
        lo, hi = ds_first // TILE, (first + 127) // TILE
        j = lax.rem(i - slot + 4, 4)
        wide = lax.broadcasted_iota(jnp.int32, (ROWS, 128), 1)
        for r in range(4):

            @pl.when(j == r)
            def _(r=r):
                q = q_refs[r]
                for h in range(4):
                    qt[h * 128 : (h + 1) * 128, :] = q[:, h * 128 : (h + 1) * 128]
                for h in range(2):
                    two = q[:, 512 + h * 128 : 512 + (h + 1) * 128].astype(f32)
                    qs[h * 256 : h * 256 + 128, :] = jnp.where(wide < 64, two, 0.0).astype(bf16)
                    qs[h * 256 + 128 : h * 256 + 256, :] = jnp.where(
                        wide < 64, pltpu.roll(two, 64, 1), 0.0
                    ).astype(bf16)

        for ref in (mt, ms):
            ref[...] = jnp.full((8, COLS), NEGATIVE, f32)
        for ref in (lt, ls):
            ref[...] = jnp.zeros((8, COLS), f32)
        for ref in (at, as_):
            ref[1] = jnp.zeros((8, COLS), f32)
        acct[...] = jnp.zeros((128, COLS), f32)
        accs[...] = jnp.zeros((64, COLS), f32)
        for ref in (pt, ps):
            ref[1] = jnp.zeros((TILE, COLS), bf16)

        def place(t):
            t = jnp.clip(t, lo, hi)
            p = t // 2
            return lax.rem(p // 4 + p, 2) * 4 + lax.rem(i - lax.rem(p, 4) + 4, 4), lax.rem(t, 2) * 4

        def keyed(ref, t):
            g, u = place(t)
            return ref[g, pl.ds(u, 4)].reshape(TILE, 128)

        def valued(ref, t):
            g, u = place(t)
            return jnp.concatenate([ref[g, u + n] for n in range(4)], axis=1)

        def half(t, c):
            o = 1 - c

            @pl.when((t * TILE < ds_last) | ((t + 1) * TILE - 1 > first))
            def _():
                kpos = t * TILE + lax.broadcasted_iota(jnp.int32, (TILE, 128), 0)
                qpos = first + lax.broadcasted_iota(jnp.int32, (TILE, 128), 1)
                ok = (kpos <= qpos) & (kpos >= doc_start(qpos))
                for ref in (st, ss):
                    for h in range(4):
                        sl = slice(h * 128, (h + 1) * 128)
                        ref[c, :, sl] = jnp.where(ok, ref[c, :, sl], NEGATIVE)

            st[o] = dot_nt(keyed(kt, t + 1), qt[...])
            softmax(st.at[c], pt.at[c], mt, lt, at.at[c], SCALE_T)
            ss[o] = dot_nt(keyed(ks, t + 1), qs[...])
            softmax(ss.at[c], ps.at[c], ms, ls, as_.at[c], SCALE_S)
            acct[...] = rescale(acct[...], at[o]) + dot_nn(valued(vt, t - 1), pt[o])
            accs[...] = rescale(accs[...], as_[o]) + dot_nn(valued(vs, t - 1), ps[o])

        st[0] = dot_nt(keyed(kt, lo), qt[...])
        ss[0] = dot_nt(keyed(ks, lo), qs[...])

        def step(n, c):
            t = lo + 2 * n
            half(t, 0)
            half(t + 1, 1)
            return c

        count = (hi - lo + 2) // 2
        lax.fori_loop(0, count, step, 0)
        last = lo + 2 * count - 1
        out_t = rescale(acct[...], at[1]) + dot_nn(valued(vt, last), pt[1])
        out_s = rescale(accs[...], as_[1]) + dot_nn(valued(vs, last), ps[1])
        for n, (out, l_ref, o_ref) in enumerate(((out_t, lt, ot_ref), (out_s, ls, os_ref))):
            out = (out / jnp.sum(l_ref[...], axis=0, keepdims=True)).astype(bf16)
            o_ref[slot] = out
            out = out.astype(f32)
            square = jnp.sum(out * out, axis=0, keepdims=True)
            square = square[:, 0:128] + square[:, 128:256] + square[:, 256:384] + square[:, 384:512]
            for d in range(PB):
                ssq_ref[pl.ds(d * 8 + n * 4 + slot, 1), :] = square
        return carry

    lax.fori_loop(0, 4, block, 0)


def attend(queries, parts):
    return pl.pallas_call(
        attend_kernel,
        out_shape=[
            jax.ShapeDtypeStruct((4, TD, COLS), bf16),
            jax.ShapeDtypeStruct((4, SD, COLS), bf16),
            jax.ShapeDtypeStruct((PB * 8, 128), f32),
        ],
        in_specs=[whole()] * 20,
        out_specs=[whole()] * 3,
        scratch_shapes=[VMEM((8, 8, 128, 128), bf16)] * 3
        + [VMEM((8, 8, 64, 128), bf16)]
        + [VMEM((COLS, 128), bf16)] * 2
        + [VMEM((2, TILE, COLS), f32)] * 2
        + [VMEM((2, TILE, COLS), bf16)] * 2
        + [VMEM((8, COLS), f32)] * 4
        + [VMEM((2, 8, COLS), f32)] * 2
        + [VMEM((TD, COLS), f32), VMEM((SD, COLS), f32)]
        + [pltpu.SemaphoreType.DMA],
        compiler_params=params(22),
        name="attend",
    )(*queries, *parts)


def distill_kernel(ot_ref, os_ref, sums_ref, w_ref, grad_ref, loss_ref):
    p, b = lax.axis_index("pb"), lax.axis_index("ha")
    sums = sums_ref[0:8, :]
    for n in range(1, PB):
        sums = sums + sums_ref[8 * n : 8 * n + 8, :]
    norm_t = lax.rsqrt(sums[0:4] / (32 * TD) + EPSILON)
    norm_s = lax.rsqrt(sums[4:8] / (32 * SD) + EPSILON)
    norm_t = jnp.concatenate([norm_t[s : s + 1] for s in range(4)], axis=1)
    norm_s = jnp.concatenate([norm_s[s : s + 1] for s in range(4)], axis=1)
    losses = jnp.zeros((1, COLS), f32)
    for h in range(4):
        sl = slice(h * 128, (h + 1) * 128)
        target = jnp.concatenate([ot_ref[s, :, sl] for s in range(4)], axis=1).astype(f32) * norm_t
        feature = jnp.concatenate([os_ref[s, :, sl] for s in range(4)], axis=1).astype(f32) * norm_s
        feature = feature.astype(bf16)
        predicted = lax.dot_general(
            w_ref[p * 4 + h], feature, (((0,), (0,)), ((), ())), preferred_element_type=f32
        )
        difference = predicted - target
        losses = losses + jnp.sum(difference * difference, axis=0, keepdims=True)
        high = difference.astype(bf16)
        low = (difference - high.astype(f32)).astype(bf16)
        grad_ref[h * 64 : (h + 1) * 64, :] = (dot_nt(feature, high) + dot_nt(feature, low)) * (
            1.0 / math.sqrt(TOKENS)
        )
    loss_ref[...] = jnp.zeros((PB * HA, 64), f32)
    for s in range(4):
        outer = jnp.where(s % 2 == b, s, s + 4)
        loss = losses[:, s * 128 : (s + 1) * 128] * (1.0 / (32 * TD))
        loss_ref[pl.ds(outer * 2, 1), :] = loss[:, 0:64]
        loss_ref[pl.ds(outer * 2 + 1, 1), :] = pltpu.roll(loss, 64, 1)[:, 0:64]


def distill(out_t, out_s, sums, weight):
    return pl.pallas_call(
        distill_kernel,
        out_shape=[jax.ShapeDtypeStruct((256, 128), f32), jax.ShapeDtypeStruct((PB * HA, 64), f32)],
        in_specs=[whole()] * 4,
        out_specs=[whole()] * 2,
        compiler_params=params(16),
        name="distill",
    )(out_t, out_s, sums, weight)


def local(teacher_q, teacher_k, teacher_v, student_q, student_k, student_v, doc_ids, proj_weight):
    keys = pack_keys(teacher_k, teacher_v, student_k, student_v, doc_ids.reshape(1, ROWS))
    own = join([permute(keys[j], to_group(j)) for j in range(4)])
    up, right, left = from_z(own), from_x(own, 1), from_x(own, -1)
    far = from_x(own, 2)
    queries = pack_queries(teacher_q, student_q)
    queries, up = lax.optimization_barrier((queries, up))
    queries = [permute(queries[j], to_group(j)) for j in range(4)]
    parts = [own, right, left, far, up, from_x(up, 1), from_x(up, -1), from_z(far)]
    parts = parts + [from_core(part) for part in parts]
    out_t, out_s, sums = attend(queries, parts)
    sums = lax.all_to_all(sums, "pb", split_axis=0, concat_axis=0, tiled=True)
    grad, loss = distill(out_t, out_s, sums, proj_weight)
    grad = lax.all_to_all(grad, ("kv", "ha"), split_axis=0, concat_axis=0, tiled=True)
    grad = jnp.sum(grad.reshape(16, 16, 128), axis=0)
    loss = lax.all_to_all(loss, ("pb", "ha"), split_axis=0, concat_axis=0, tiled=True)
    return grad, jnp.sum(loss, axis=0)


def solution(mesh):
    in_specs = (
        P(("pb", "kv"), "ha"),
        P(("pb", "kv"), "ha"),
        P(("pb", "kv"), "ha"),
        P(("pb", "kv"), "ha"),
        P(("pb", "kv"), "ha"),
        P(("pb", "kv"), "ha"),
        P(("pb", "kv")),
        P(),
    )
    out_specs = (P(("pb", "kv", "ha"), None), P(("pb", "kv", "ha")))
    return jax.shard_map(local, mesh=mesh, in_specs=in_specs, out_specs=out_specs, check_vma=False)
```

```python
import functools
import math

import jax
import jax.numpy as jnp
from jax import lax
from jax.experimental import pallas as pl
from jax.experimental.pallas import tpu as pltpu
from jax.sharding import PartitionSpec as P

TD = 128
SD = 64
PB, KV, HA = 8, 8, 2
ROWS = 128
PAD = 16
BLOCK = ROWS + PAD
UNIT = 4 * ROWS + PAD
STATS = 24
TOKENS = PB * KV * ROWS
COLS = 512
ALL = ("pb", "kv", "ha")
NEGATIVE = -1e30
EPSILON = 1e-06
LOG2E = 1.4426950408889634
SCALE_T = LOG2E / math.sqrt(TD)
SCALE_S = LOG2E / math.sqrt(SD)
f32 = jnp.float32
bf16 = jnp.bfloat16
VMEM = pltpu.VMEM


def index(pb, kv, ha):
    return (pb * KV + kv) * HA + ha


def core_of(p):
    return (p // 4 + p) % 2


def permute(x, move):
    pairs = [
        (index(p, k, a), index(*move(p, k, a))) for p in range(PB) for k in range(KV) for a in range(HA)
    ]
    return lax.ppermute(x, ALL, pairs)


def from_x(x, step):
    return permute(x, lambda p, k, a: (p, (((k // 2) - step) % 4) * 2 + k % 2, a))


def from_z(x):
    return permute(x, lambda p, k, a: (p, k ^ 1, a))


def from_core(x):
    return permute(x, lambda p, k, a: (p, k, 1 - a))


def to_group(j):
    return lambda p, k, a: (4 * a + (j + p) % 4, k, core_of(p))


def params(mib):
    return pltpu.CompilerParams(vmem_limit_bytes=mib * 1024 * 1024)


def whole(space=None):
    return pl.BlockSpec(memory_space=VMEM if space is None else space)


def bring(pairs, sem):
    copies = [pltpu.make_async_copy(src, dst, sem.at[n]) for n, (src, dst) in enumerate(pairs)]
    for c in copies:
        c.start()
    for c in copies:
        c.wait()


def pack_kernel(tk_, tv_, sk_, sv_, doc_, o0, o1, o2, o3, tk, tv, sk, sv, doc, sem):
    bring([(tk_, tk), (tv_, tv), (sk_, sk), (sv_, sv), (doc_, doc)], sem)
    p = lax.axis_index("pb")
    lane = lax.broadcasted_iota(jnp.int32, (ROWS, 128), 1)
    row = lax.broadcasted_iota(jnp.int32, (PAD, 384), 0)
    ids = doc[...]
    counts = [jnp.sum(jnp.where(ids < d, 1.0, 0.0), axis=1, keepdims=True) for d in (1, 2, 3)]
    for j, out in enumerate((o0, o1, o2, o3)):
        i = lax.rem(p + j, 4)
        odd = lax.rem(i, 2) == 1
        at = pl.ds(pl.multiple_of(i * 128, 128), 128)
        pair = pl.ds(pl.multiple_of((i // 2) * 128, 128), 128)
        out[0:ROWS, 0:128] = tk[:, at]
        out[0:ROWS, 128:256] = tv[:, at].astype(f32).T.astype(bf16)
        keys = sk[:, pair].astype(f32)
        keys = jnp.where(odd, pltpu.roll(keys, 64, 1), keys)
        values = sv[:, pair].astype(f32).T
        values = jnp.where(odd, values[64:128], values[0:64])
        values = jnp.concatenate([pltpu.roll(values, 64, 1), values], axis=0)
        out[0:ROWS, 256:384] = jnp.where(lane < 64, keys, values).astype(bf16)
        pad = jnp.zeros((PAD, 384), f32)
        for d in (1, 2, 3):
            pad = jnp.where(row == 4 * j + d, counts[d - 1], pad)
        out[ROWS:BLOCK, :] = pad.astype(bf16)


def pack_queries_kernel(tq_, sq_, o0, o1, o2, o3, tq, sq, sem):
    bring([(tq_, tq), (sq_, sq)], sem)
    p = lax.axis_index("pb")
    for j, out in enumerate((o0, o1, o2, o3)):
        i = lax.rem(p + j, 4)
        out[:, 0:512] = tq[:, pl.ds(pl.multiple_of(i * 512, 512), 512)]
        out[:, 512:768] = sq[:, pl.ds(pl.multiple_of(i * 256, 256), 256)]


def pack(kernel, shape, *args):
    return pl.pallas_call(
        kernel,
        out_shape=[jax.ShapeDtypeStruct(shape, bf16)] * 4,
        in_specs=[whole(pl.ANY)] * len(args),
        out_specs=[whole()] * 4,
        scratch_shapes=[VMEM(x.shape, x.dtype) for x in args] + [pltpu.SemaphoreType.DMA((len(args),))],
        compiler_params=params(56),
        name="pack",
    )(*args)


def join_kernel(r0, r1, r2, r3, out):
    pad = jnp.zeros((PAD, 384), f32)
    for j, r in enumerate((r0, r1, r2, r3)):
        out[j * ROWS : (j + 1) * ROWS, :] = r[0:ROWS, :]
        pad = pad + r[ROWS:BLOCK, :].astype(f32)
    out[4 * ROWS : UNIT, :] = pad.astype(bf16)


def join(rounds):
    return pl.pallas_call(
        join_kernel,
        out_shape=jax.ShapeDtypeStruct((UNIT, 384), bf16),
        in_specs=[whole()] * 4,
        out_specs=whole(),
        compiler_params=params(8),
        name="join",
    )(*rounds)


def dot_nt(a, b):
    return lax.dot_general(a, b, (((1,), (1,)), ((), ())), preferred_element_type=f32)


def dot_nn(a, b):
    return lax.dot_general(a, b, (((1,), (0,)), ((), ())), preferred_element_type=f32)


def dot_tn(a, b):
    return lax.dot_general(a, b, (((0,), (0,)), ((), ())), preferred_element_type=f32)


def attend_kernel(units, *refs):
    size = len(units)
    tile = 128 * size
    refs = list(refs)

    def take(n):
        out = refs[:n]
        del refs[:n]
        return out

    q_refs = take(4)
    own_parts = take(size)
    other_parts = take(size)
    weight, ot_ref, os_ref, stat_ref = take(4)
    mt, ms, acct, accs, kt, vt, ks, vs, plan, qt, qs, st, ss, pt, ps, at, as_ = refs
    pb, k, b = lax.axis_index("pb"), lax.axis_index("kv"), lax.axis_index("ha")
    i, x, z = pb & 3, k >> 1, k & 1
    chips = []
    for unit in units:
        dx = (0, 1, 3, 2)[unit % 4]
        chips.append(((x + dx) & 3) * 2 + (z if unit < 4 else 1 - z))
    lane = lax.broadcasted_iota(jnp.int32, (64, 128), 1)
    wide = lax.broadcasted_iota(jnp.int32, (ROWS, 128), 1)
    total = jnp.zeros((PAD, 128), f32)
    for side, parts in ((b, own_parts), (1 - b, other_parts)):
        for u, part in enumerate(parts):
            cols = slice(u * 128, (u + 1) * 128)
            for j in range(4):
                rows = slice(j * ROWS, (j + 1) * ROWS)
                g = side * 4 + j
                kt[g, cols, :] = part[rows, 0:128]
                vt[g, 0:TD, cols] = part[rows, 128:256]
                both = part[rows, 256:384]
                ks[g, cols, :] = both
                both = both.astype(f32)
                vs[g, 0:SD, cols] = jnp.where(lane < 64, pltpu.roll(both[0:64], 64, 1), both[64:128]).astype(bf16)
            total = total + part[4 * ROWS : UNIT, 0:128].astype(f32)
    starts = []
    for d in (1, 2, 3):
        row = total[d : d + 1] + total[d + 4 : d + 5] + total[d + 8 : d + 9] + total[d + 12 : d + 13]
        starts.append(jnp.max(row).astype(jnp.int32))
    for g in range(8):
        vt[g, TD : TD + 16, :] = jnp.ones((16, tile), bf16)
        vs[g, SD : SD + 16, :] = jnp.ones((16, tile), bf16)
    for j in range(4):
        slot = (i - j) & 3
        q = q_refs[j]
        for h in range(4):
            qt[slot, h * 128 : (h + 1) * 128, :] = q[:, h * 128 : (h + 1) * 128]
        for h in range(2):
            two = q[:, 512 + h * 128 : 640 + h * 128].astype(f32)
            qs[slot, h * 256 : h * 256 + 128, :] = jnp.where(wide < 64, two, 0.0).astype(bf16)
            qs[slot, h * 256 + 128 : h * 256 + 256, :] = jnp.where(wide < 64, pltpu.roll(two, 64, 1), 0.0).astype(
                bf16
            )
    for ref in (mt, ms):
        ref[...] = jnp.full((4, 8, COLS), NEGATIVE, f32)
    for ref in (acct, accs):
        ref[...] = jnp.zeros(ref.shape, f32)
    for ref in (at, as_):
        ref[1] = jnp.ones((8, COLS), f32)
    for ref in (pt, ps):
        ref[1] = jnp.zeros((tile, COLS), bf16)

    def doc_start(pos):
        at_ = jnp.where(pos >= starts[0], starts[0], 0)
        at_ = jnp.where(pos >= starts[1], starts[1], at_)
        return jnp.where(pos >= starts[2], starts[2], at_)

    count = jnp.int32(0)
    for slot in range(4):
        p = jnp.where(slot % 2 == b, slot, slot + 4)
        first = p * 1024 + k * 128

        def enter(t, count, slot=slot, first=first):
            plan[0, count + 1] = jnp.int32(slot)
            plan[1, count + 1] = t
            plan[2, count + 1] = (((t >> 2) + t) & 1) * 4 + ((i - t) & 3)
            plan[3, count + 1] = first
            return count + 1

        count = lax.fori_loop(doc_start(first) >> 10, p + 1, enter, count)
    for n in (0, 2):
        plan[n, 0] = plan[n, 1]
        plan[n, count + 1] = plan[n, count]

    def softmax(s_ref, p_ref, m_ref, a_ref, scale):
        old = m_ref[...]
        top = None
        for r in range(0, tile, 64):
            s = jnp.max(s_ref[r : r + 64, :].reshape(8, 8, COLS), axis=0)
            top = s if top is None else jnp.maximum(top, s)
        new = jnp.maximum(old, jnp.max(top, axis=0, keepdims=True))
        for r in range(0, tile, 64):
            w = jnp.exp2((s_ref[r : r + 64, :].reshape(8, 8, COLS) - new[None]) * scale)
            p_ref[r : r + 64, :] = w.reshape(64, COLS).astype(bf16)
        a_ref[...] = jnp.exp2((old - new) * scale)
        m_ref[...] = new

    def rescale(acc, a):
        n = acc.shape[0] // 8
        return (acc.reshape(n, 8, COLS) * a[None]).reshape(n * 8, COLS)

    def mask(n, c):
        tile_at, first = plan[1, n] * 1024, plan[3, n]
        ds_first, ds_last = doc_start(first), doc_start(first + 127)

        @pl.when((tile_at < ds_last) | (tile_at + 1023 > first))
        def _():
            for u in range(size):
                rows = slice(u * 128, (u + 1) * 128)
                at_ = tile_at + chips[u] * 128
                outside = (at_ + 127 < ds_first) | (at_ > first + 127)

                @pl.when(outside)
                def _(rows=rows):
                    for ref in (st, ss):
                        ref[c, rows, :] = jnp.full((128, COLS), NEGATIVE, f32)

                @pl.when(jnp.logical_not(outside) & ((at_ < ds_last) | (at_ + 127 > first)))
                def _(rows=rows, at_=at_):
                    qpos = first + lax.broadcasted_iota(jnp.int32, (128, 128), 1)
                    kpos = at_ + lax.broadcasted_iota(jnp.int32, (128, 128), 0)
                    ok = (kpos <= qpos) & (kpos >= doc_start(qpos))
                    for ref in (st, ss):
                        for h in range(4):
                            sl = slice(h * 128, (h + 1) * 128)
                            ref[c, rows, sl] = jnp.where(ok, ref[c, rows, sl], NEGATIVE)

    def queries_by_keys(n, c):
        slot, g = plan[0, n], plan[2, n]
        st[c] = dot_nt(kt[g], qt[slot])
        ss[c] = dot_nt(ks[g], qs[slot])

    def add_values(n, c):
        slot, g = plan[0, n], plan[2, n]
        acct[slot] = rescale(acct[slot], at[c]) + dot_nn(vt[g], pt[c])
        accs[slot] = rescale(accs[slot], as_[c]) + dot_nn(vs[g], ps[c])

    def half(n, c):
        mask(n, c)
        slot, after, g = plan[0, n], plan[0, n + 1], plan[2, n + 1]
        st[1 - c] = dot_nt(kt[g], qt[after])
        softmax(st.at[c], pt.at[c], mt.at[slot], at.at[c], SCALE_T)
        ss[1 - c] = dot_nt(ks[g], qs[after])
        softmax(ss.at[c], ps.at[c], ms.at[slot], as_.at[c], SCALE_S)
        add_values(n - 1, 1 - c)

    queries_by_keys(1, 0)

    def step(n, c):
        half(2 * n + 1, 0)
        half(2 * n + 2, 1)
        return c

    lax.fori_loop(0, count >> 1, step, 0)
    odd = (count & 1) == 1

    @pl.when(odd)
    def _():
        half(count, 0)
        add_values(count, 0)

    @pl.when(jnp.logical_not(odd))
    def _():
        add_values(count, 1)

    base = pb * 4
    for slot in range(4):
        out_t = (acct[slot, 0:TD, :] / acct[slot, TD : TD + 1, :]).astype(bf16)
        out_s = (accs[slot, 0:SD, :] / accs[slot, SD : SD + 1, :]).astype(bf16)
        ot_ref[slot] = out_t
        os_ref[slot] = out_s
        targets = [out_t[:, h * 128 : (h + 1) * 128].astype(f32) for h in range(4)]
        students = [out_s[:, h * 128 : (h + 1) * 128] for h in range(4)]
        predicted = [dot_tn(weight[base + h], students[h]) for h in range(4)]

        def across(pieces):
            total = pieces[0]
            for piece in pieces[1:]:
                total = total + piece
            return jnp.sum(total, axis=0, keepdims=True)

        sum_t = across([t * t for t in targets])
        sum_s = across([s.astype(f32) * s.astype(f32) for s in students])
        cross = across([y * t for y, t in zip(predicted, targets)])
        kappa = jnp.where(sum_t > 0.0, cross / jnp.where(sum_t > 0.0, sum_t, 1.0), 0.0)
        rest = [y - kappa * t for y, t in zip(predicted, targets)]
        sum_e = across([y * y for y in rest])
        sum_x = across([y * t for y, t in zip(rest, targets)])
        for n, value in enumerate((sum_t, sum_s, kappa, sum_e, sum_x)):
            for d in range(PB):
                stat_ref[d * STATS + n * 4 + slot : d * STATS + n * 4 + slot + 1, :] = value
    for d in range(PB):
        stat_ref[d * STATS + 20 : (d + 1) * STATS, :] = jnp.zeros((STATS - 20, 128), f32)


def attend(queries, own_parts, other_parts, weight):
    size = len(own_parts)
    tile = 128 * size
    args = [*queries, *own_parts, *other_parts, weight]
    return pl.pallas_call(
        functools.partial(attend_kernel, tuple(range(size))),
        out_shape=[
            jax.ShapeDtypeStruct((4, TD, COLS), bf16),
            jax.ShapeDtypeStruct((4, SD, COLS), bf16),
            jax.ShapeDtypeStruct((PB * STATS, 128), f32),
        ],
        in_specs=[whole()] * len(args),
        out_specs=[whole()] * 3,
        scratch_shapes=[VMEM((4, 8, COLS), f32)] * 2
        + [
            VMEM((4, TD + 16, COLS), f32),
            VMEM((4, SD + 16, COLS), f32),
            VMEM((8, tile, 128), bf16),
            VMEM((8, TD + 16, tile), bf16),
            VMEM((8, tile, 128), bf16),
            VMEM((8, SD + 16, tile), bf16),
            pltpu.SMEM((4, 40), jnp.int32),
        ]
        + [VMEM((4, COLS, 128), bf16)] * 2
        + [VMEM((2, tile, COLS), f32)] * 2
        + [VMEM((2, tile, COLS), bf16)] * 2
        + [VMEM((2, 8, COLS), f32)] * 2,
        compiler_params=params(40),
        name="attend",
    )(*args)


def distill_kernel(ot_ref, os_ref, stat_ref, w_ref, grad_ref, loss_ref):
    p, b = lax.axis_index("pb"), lax.axis_index("ha")

    def stat(n, d):
        return stat_ref[d * STATS + 4 * n : d * STATS + 4 * n + 4, :]

    sum_t, sum_s = stat(0, 0), stat(1, 0)
    for d in range(1, PB):
        sum_t, sum_s = sum_t + stat(0, d), sum_s + stat(1, d)
    norm_t = lax.rsqrt(sum_t / (32 * TD) + EPSILON)
    norm_s = lax.rsqrt(sum_s / (32 * SD) + EPSILON)
    ratio = norm_t / norm_s
    loss = jnp.zeros((4, 128), f32)
    for d in range(PB):
        off = stat(2, d) - ratio
        loss = loss + (stat(3, d) + 2.0 * off * stat(4, d) + (off * stat(0, d)) * off)
    loss_ref[...] = loss * (norm_s * norm_s) * (1.0 / (32 * TD))
    norm_t = jnp.concatenate([norm_t[s : s + 1] for s in range(4)], axis=1)
    norm_s = jnp.concatenate([norm_s[s : s + 1] for s in range(4)], axis=1)
    for h in range(4):
        sl = slice(h * 128, (h + 1) * 128)
        target = jnp.concatenate([ot_ref[s, :, sl] for s in range(4)], axis=1).astype(f32) * norm_t
        feature = jnp.concatenate([os_ref[s, :, sl] for s in range(4)], axis=1).astype(f32) * norm_s
        feature = feature.astype(bf16)
        difference = dot_tn(w_ref[p * 4 + h], feature) - target
        high = difference.astype(bf16)
        low = (difference - high.astype(f32)).astype(bf16)
        grad_ref[h * 64 : (h + 1) * 64, :] = (dot_nt(feature, high) + dot_nt(feature, low)) * (
            1.0 / math.sqrt(TOKENS)
        )


def distill(out_t, out_s, stats, weight):
    return pl.pallas_call(
        distill_kernel,
        out_shape=[jax.ShapeDtypeStruct((256, 128), f32), jax.ShapeDtypeStruct((4, 128), f32)],
        in_specs=[whole()] * 4,
        out_specs=[whole()] * 2,
        compiler_params=params(16),
        name="distill",
    )(out_t, out_s, stats, weight)


def local(teacher_q, teacher_k, teacher_v, student_q, student_k, student_v, doc_ids, proj_weight):
    p, a = lax.axis_index("pb"), lax.axis_index("ha")
    sent = pack(
        pack_kernel, (BLOCK, 384), teacher_k, teacher_v, student_k, student_v, doc_ids.reshape(1, ROWS)
    )
    rounds = [permute(sent[j], to_group(j)) for j in range(4)]
    own = join(rounds)
    up = from_z(own)
    far = from_x(own, 2)
    right, left = from_x(own, 1), from_x(own, -1)
    queries = pack(pack_queries_kernel, (ROWS, 768), teacher_q, student_q)
    swapped = {0: from_core(own)}
    queries, swapped[0] = lax.optimization_barrier((queries, swapped[0]))
    queries = [permute(queries[j], to_group(j)) for j in range(4)]
    parts = [own, right, left, far, up, from_x(up, 1), from_x(up, -1), from_z(far)]
    others = [swapped[u] if u in swapped else from_core(parts[u]) for u in range(8)]
    out_t, out_s, stats = attend(queries, parts, others, proj_weight)
    stats = lax.all_to_all(stats, "pb", split_axis=0, concat_axis=0, tiled=True)
    grad, loss = distill(out_t, out_s, stats, proj_weight)
    other = from_core(loss)
    loss = jnp.where((p // 4 + p) % 2 == a, loss, other)
    loss = lax.dynamic_slice(loss, (p % 4, a * 64), (1, 64)).reshape(64)
    grad = lax.all_to_all(grad, ("kv", "ha"), split_axis=0, concat_axis=0, tiled=True)
    return jnp.sum(grad.reshape(16, 16, 128), axis=0), loss


def solution(mesh):
    in_specs = (
        P(("pb", "kv"), "ha"),
        P(("pb", "kv"), "ha"),
        P(("pb", "kv"), "ha"),
        P(("pb", "kv"), "ha"),
        P(("pb", "kv"), "ha"),
        P(("pb", "kv"), "ha"),
        P(("pb", "kv")),
        P(),
    )
    out_specs = (P(("pb", "kv", "ha"), None), P(("pb", "kv", "ha")))
    return jax.shard_map(local, mesh=mesh, in_specs=in_specs, out_specs=out_specs, check_vma=False)
```

```python
import functools
import math

import jax
import jax.numpy as jnp
from jax import lax
from jax.experimental import pallas as pl
from jax.experimental.pallas import tpu as pltpu
from jax.sharding import PartitionSpec as P

TD = 128
SD = 64
PB, KV, HA = 8, 8, 2
ROWS = 128
PAD = 16
BLOCK = ROWS + PAD
UNIT = 4 * ROWS + PAD
STATS = 24
TOKENS = PB * KV * ROWS
COLS = 512
ALL = ("pb", "kv", "ha")
NEGATIVE = -1e30
EPSILON = 1e-06
LOG2E = 1.4426950408889634
SCALE_T = LOG2E / math.sqrt(TD)
SCALE_S = LOG2E / math.sqrt(SD)
f32 = jnp.float32
bf16 = jnp.bfloat16
VMEM = pltpu.VMEM


def index(pb, kv, ha):
    return (pb * KV + kv) * HA + ha


def core_of(p):
    return (p // 4 + p) % 2


def permute(x, move):
    pairs = [
        (index(p, k, a), index(*move(p, k, a))) for p in range(PB) for k in range(KV) for a in range(HA)
    ]
    return lax.ppermute(x, ALL, pairs)


def from_x(x, step):
    return permute(x, lambda p, k, a: (p, (((k // 2) - step) % 4) * 2 + k % 2, a))


def from_z(x):
    return permute(x, lambda p, k, a: (p, k ^ 1, a))


def from_core(x):
    return permute(x, lambda p, k, a: (p, k, 1 - a))


def to_group(j):
    return lambda p, k, a: (4 * a + (j + p) % 4, k, core_of(p))


def params(mib):
    return pltpu.CompilerParams(vmem_limit_bytes=mib * 1024 * 1024)


def whole(space=None):
    return pl.BlockSpec(memory_space=VMEM if space is None else space)


def bring(pairs, sem):
    copies = [pltpu.make_async_copy(src, dst, sem.at[n]) for n, (src, dst) in enumerate(pairs)]
    for c in copies:
        c.start()
    for c in copies:
        c.wait()


def pack_kernel(tk_, tv_, sk_, sv_, doc_, o0, o1, o2, o3, tk, tv, sk, sv, doc, sem):
    bring([(tk_, tk), (tv_, tv), (sk_, sk), (sv_, sv), (doc_, doc)], sem)
    p = lax.axis_index("pb")
    lane = lax.broadcasted_iota(jnp.int32, (ROWS, 128), 1)
    row = lax.broadcasted_iota(jnp.int32, (PAD, 384), 0)
    ids = doc[...]
    counts = [jnp.sum(jnp.where(ids < d, 1.0, 0.0), axis=1, keepdims=True) for d in (1, 2, 3)]
    for j, out in enumerate((o0, o1, o2, o3)):
        i = lax.rem(p + j, 4)
        odd = lax.rem(i, 2) == 1
        at = pl.ds(pl.multiple_of(i * 128, 128), 128)
        pair = pl.ds(pl.multiple_of((i // 2) * 128, 128), 128)
        out[0:ROWS, 0:128] = tk[:, at]
        out[0:ROWS, 128:256] = tv[:, at].astype(f32).T.astype(bf16)
        keys = sk[:, pair].astype(f32)
        keys = jnp.where(odd, pltpu.roll(keys, 64, 1), keys)
        values = sv[:, pair].astype(f32).T
        values = jnp.where(odd, values[64:128], values[0:64])
        values = jnp.concatenate([pltpu.roll(values, 64, 1), values], axis=0)
        out[0:ROWS, 256:384] = jnp.where(lane < 64, keys, values).astype(bf16)
        pad = jnp.zeros((PAD, 384), f32)
        for d in (1, 2, 3):
            pad = jnp.where(row == 4 * j + d, counts[d - 1], pad)
        out[ROWS:BLOCK, :] = pad.astype(bf16)


def pack_queries_kernel(tq_, sq_, o0, o1, o2, o3, tq, sq, sem):
    bring([(tq_, tq), (sq_, sq)], sem)
    p = lax.axis_index("pb")
    for j, out in enumerate((o0, o1, o2, o3)):
        i = lax.rem(p + j, 4)
        out[:, 0:512] = tq[:, pl.ds(pl.multiple_of(i * 512, 512), 512)]
        out[:, 512:768] = sq[:, pl.ds(pl.multiple_of(i * 256, 256), 256)]


def pack(kernel, shape, *args):
    return pl.pallas_call(
        kernel,
        out_shape=[jax.ShapeDtypeStruct(shape, bf16)] * 4,
        in_specs=[whole(pl.ANY)] * len(args),
        out_specs=[whole()] * 4,
        scratch_shapes=[VMEM(x.shape, x.dtype) for x in args] + [pltpu.SemaphoreType.DMA((len(args),))],
        compiler_params=params(56),
        name="pack",
    )(*args)


def join_kernel(r0, r1, r2, r3, out):
    pad = jnp.zeros((PAD, 384), f32)
    for j, r in enumerate((r0, r1, r2, r3)):
        out[j * ROWS : (j + 1) * ROWS, :] = r[0:ROWS, :]
        pad = pad + r[ROWS:BLOCK, :].astype(f32)
    out[4 * ROWS : UNIT, :] = pad.astype(bf16)


def join(rounds):
    return pl.pallas_call(
        join_kernel,
        out_shape=jax.ShapeDtypeStruct((UNIT, 384), bf16),
        in_specs=[whole()] * 4,
        out_specs=whole(),
        compiler_params=params(8),
        name="join",
    )(*rounds)


def dot_nt(a, b):
    return lax.dot_general(a, b, (((1,), (1,)), ((), ())), preferred_element_type=f32)


def dot_nn(a, b):
    return lax.dot_general(a, b, (((1,), (0,)), ((), ())), preferred_element_type=f32)


def dot_tn(a, b):
    return lax.dot_general(a, b, (((0,), (0,)), ((), ())), preferred_element_type=f32)


def attend_kernel(units, *refs):
    size = len(units)
    tile = 128 * size
    refs = list(refs)

    def take(n):
        out = refs[:n]
        del refs[:n]
        return out

    q_refs = take(4)
    own_parts = take(size)
    other_parts = take(size)
    weight, ot_ref, os_ref, stat_ref = take(4)
    mt, ms, acct, accs, kt, vt, ks, vs, plan, qt, qs, st, ss, pt, ps, at, as_ = refs
    pb, k, b = lax.axis_index("pb"), lax.axis_index("kv"), lax.axis_index("ha")
    i, x, z = pb & 3, k >> 1, k & 1
    chips = []
    for unit in units:
        dx = (0, 1, 3, 2)[unit % 4]
        chips.append(((x + dx) & 3) * 2 + (z if unit < 4 else 1 - z))
    lane = lax.broadcasted_iota(jnp.int32, (64, 128), 1)
    wide = lax.broadcasted_iota(jnp.int32, (ROWS, 128), 1)
    total = jnp.zeros((PAD, 128), f32)
    for side, parts in ((b, own_parts), (1 - b, other_parts)):
        for u, part in enumerate(parts):
            cols = slice(u * 128, (u + 1) * 128)
            for j in range(4):
                rows = slice(j * ROWS, (j + 1) * ROWS)
                g = side * 4 + j
                kt[g, cols, :] = part[rows, 0:128]
                vt[g, 0:TD, cols] = part[rows, 128:256]
                both = part[rows, 256:384]
                ks[g, cols, :] = both
                both = both.astype(f32)
                vs[g, 0:SD, cols] = jnp.where(lane < 64, pltpu.roll(both[0:64], 64, 1), both[64:128]).astype(bf16)
            total = total + part[4 * ROWS : UNIT, 0:128].astype(f32)
    starts = []
    for d in (1, 2, 3):
        row = total[d : d + 1] + total[d + 4 : d + 5] + total[d + 8 : d + 9] + total[d + 12 : d + 13]
        starts.append(jnp.max(row).astype(jnp.int32))
    for g in range(8):
        vt[g, TD : TD + 16, :] = jnp.ones((16, tile), bf16)
        vs[g, SD : SD + 16, :] = jnp.ones((16, tile), bf16)
    for j in range(4):
        slot = (i - j) & 3
        q = q_refs[j]
        for h in range(4):
            qt[slot, h * 128 : (h + 1) * 128, :] = q[:, h * 128 : (h + 1) * 128]
        for h in range(2):
            two = q[:, 512 + h * 128 : 640 + h * 128].astype(f32)
            qs[slot, h * 256 : h * 256 + 128, :] = jnp.where(wide < 64, two, 0.0).astype(bf16)
            qs[slot, h * 256 + 128 : h * 256 + 256, :] = jnp.where(wide < 64, pltpu.roll(two, 64, 1), 0.0).astype(
                bf16
            )
    for ref in (mt, ms):
        ref[...] = jnp.full((4, 8, COLS), NEGATIVE, f32)
    for ref in (acct, accs):
        ref[...] = jnp.zeros(ref.shape, f32)
    for ref in (at, as_):
        ref[1] = jnp.ones((8, COLS), f32)
    for ref in (pt, ps):
        ref[1] = jnp.zeros((tile, COLS), bf16)

    def doc_start(pos):
        at_ = jnp.where(pos >= starts[0], starts[0], 0)
        at_ = jnp.where(pos >= starts[1], starts[1], at_)
        return jnp.where(pos >= starts[2], starts[2], at_)

    count = jnp.int32(0)
    for slot in range(4):
        p = jnp.where(slot % 2 == b, slot, slot + 4)
        first = p * 1024 + k * 128

        def enter(t, count, slot=slot, first=first):
            plan[0, count + 1] = jnp.int32(slot)
            plan[1, count + 1] = t
            plan[2, count + 1] = (((t >> 2) + t) & 1) * 4 + ((i - t) & 3)
            plan[3, count + 1] = first
            return count + 1

        count = lax.fori_loop(doc_start(first) >> 10, p + 1, enter, count)
    for n in (0, 2):
        plan[n, 0] = plan[n, 1]
        plan[n, count + 1] = plan[n, count]

    def softmax(s_ref, p_ref, m_ref, a_ref, scale):
        old = m_ref[...]
        top = None
        for r in range(0, tile, 64):
            s = jnp.max(s_ref[r : r + 64, :].reshape(8, 8, COLS), axis=0)
            top = s if top is None else jnp.maximum(top, s)
        new = jnp.maximum(old, jnp.max(top, axis=0, keepdims=True))
        for r in range(0, tile, 64):
            w = jnp.exp2((s_ref[r : r + 64, :].reshape(8, 8, COLS) - new[None]) * scale)
            p_ref[r : r + 64, :] = w.reshape(64, COLS).astype(bf16)
        a_ref[...] = jnp.exp2((old - new) * scale)
        m_ref[...] = new

    def rescale(acc, a):
        n = acc.shape[0] // 8
        return (acc.reshape(n, 8, COLS) * a[None]).reshape(n * 8, COLS)

    def mask(n, c):
        slot, tile_at, first = plan[0, n], plan[1, n] * 1024, plan[3, n]
        ds_first, ds_last = doc_start(first), doc_start(first + 127)
        newest = tile_at + 1023 > first

        @pl.when(newest & (ds_last > first))
        def _():
            column = first + (lax.broadcasted_iota(jnp.int32, (8, COLS), 1) & 127)
            for ref in (mt, ms):
                ref[slot] = jnp.where(doc_start(column) > first, NEGATIVE, ref[slot])

        @pl.when((tile_at < ds_first) | newest)
        def _():
            oldest = jnp.where(newest, ds_last, ds_first)
            for u in range(size):
                rows = slice(u * 128, (u + 1) * 128)
                at_ = tile_at + chips[u] * 128
                outside = (at_ + 127 < ds_first) | (at_ > first + 127)

                @pl.when(outside)
                def _(rows=rows):
                    for ref in (st, ss):
                        ref[c, rows, :] = jnp.full((128, COLS), NEGATIVE, f32)

                @pl.when(jnp.logical_not(outside) & ((at_ < oldest) | (at_ + 127 > first)))
                def _(rows=rows, at_=at_):
                    qpos = first + lax.broadcasted_iota(jnp.int32, (128, 128), 1)
                    kpos = at_ + lax.broadcasted_iota(jnp.int32, (128, 128), 0)
                    ok = (kpos <= qpos) & (kpos >= doc_start(qpos))
                    for ref in (st, ss):
                        for h in range(4):
                            sl = slice(h * 128, (h + 1) * 128)
                            ref[c, rows, sl] = jnp.where(ok, ref[c, rows, sl], NEGATIVE)

    def queries_by_keys(n, c):
        slot, g = plan[0, n], plan[2, n]
        st[c] = dot_nt(kt[g], qt[slot])
        ss[c] = dot_nt(ks[g], qs[slot])

    def add_values(n, c):
        slot, g = plan[0, n], plan[2, n]
        acct[slot] = rescale(acct[slot], at[c]) + dot_nn(vt[g], pt[c])
        accs[slot] = rescale(accs[slot], as_[c]) + dot_nn(vs[g], ps[c])

    def half(n, c):
        mask(n, c)
        slot, after, g = plan[0, n], plan[0, n + 1], plan[2, n + 1]
        st[1 - c] = dot_nt(kt[g], qt[after])
        softmax(st.at[c], pt.at[c], mt.at[slot], at.at[c], SCALE_T)
        ss[1 - c] = dot_nt(ks[g], qs[after])
        softmax(ss.at[c], ps.at[c], ms.at[slot], as_.at[c], SCALE_S)
        add_values(n - 1, 1 - c)

    queries_by_keys(1, 0)

    def step(n, c):
        half(2 * n + 1, 0)
        half(2 * n + 2, 1)
        return c

    lax.fori_loop(0, count >> 1, step, 0)
    odd = (count & 1) == 1

    @pl.when(odd)
    def _():
        half(count, 0)
        add_values(count, 0)

    @pl.when(jnp.logical_not(odd))
    def _():
        add_values(count, 1)

    base = pb * 4
    for slot in range(4):
        out_t = (acct[slot, 0:TD, :] / acct[slot, TD : TD + 1, :]).astype(bf16)
        out_s = (accs[slot, 0:SD, :] / accs[slot, SD : SD + 1, :]).astype(bf16)
        ot_ref[slot] = out_t
        os_ref[slot] = out_s
        targets = [out_t[:, h * 128 : (h + 1) * 128].astype(f32) for h in range(4)]
        students = [out_s[:, h * 128 : (h + 1) * 128] for h in range(4)]
        predicted = [dot_tn(weight[base + h], students[h]) for h in range(4)]

        def across(pieces):
            total = pieces[0]
            for piece in pieces[1:]:
                total = total + piece
            return jnp.sum(total, axis=0, keepdims=True)

        sum_t = across([t * t for t in targets])
        sum_s = across([s.astype(f32) * s.astype(f32) for s in students])
        cross = across([y * t for y, t in zip(predicted, targets)])
        kappa = jnp.where(sum_t > 0.0, cross / jnp.where(sum_t > 0.0, sum_t, 1.0), 0.0)
        rest = [y - kappa * t for y, t in zip(predicted, targets)]
        sum_e = across([y * y for y in rest])
        sum_x = across([y * t for y, t in zip(rest, targets)])
        for n, value in enumerate((sum_t, sum_s, kappa, sum_e, sum_x)):
            for d in range(PB):
                stat_ref[d * STATS + n * 4 + slot : d * STATS + n * 4 + slot + 1, :] = value
    for d in range(PB):
        stat_ref[d * STATS + 20 : (d + 1) * STATS, :] = jnp.zeros((STATS - 20, 128), f32)


def attend(queries, own_parts, other_parts, weight):
    size = len(own_parts)
    tile = 128 * size
    args = [*queries, *own_parts, *other_parts, weight]
    return pl.pallas_call(
        functools.partial(attend_kernel, tuple(range(size))),
        out_shape=[
            jax.ShapeDtypeStruct((4, TD, COLS), bf16),
            jax.ShapeDtypeStruct((4, SD, COLS), bf16),
            jax.ShapeDtypeStruct((PB * STATS, 128), f32),
        ],
        in_specs=[whole()] * len(args),
        out_specs=[whole()] * 3,
        scratch_shapes=[VMEM((4, 8, COLS), f32)] * 2
        + [
            VMEM((4, TD + 16, COLS), f32),
            VMEM((4, SD + 16, COLS), f32),
            VMEM((8, tile, 128), bf16),
            VMEM((8, TD + 16, tile), bf16),
            VMEM((8, tile, 128), bf16),
            VMEM((8, SD + 16, tile), bf16),
            pltpu.SMEM((4, 40), jnp.int32),
        ]
        + [VMEM((4, COLS, 128), bf16)] * 2
        + [VMEM((2, tile, COLS), f32)] * 2
        + [VMEM((2, tile, COLS), bf16)] * 2
        + [VMEM((2, 8, COLS), f32)] * 2,
        compiler_params=params(40),
        name="attend",
    )(*args)


def distill_kernel(ot_ref, os_ref, stat_ref, w_ref, grad_ref, loss_ref):
    p, b = lax.axis_index("pb"), lax.axis_index("ha")

    def stat(n, d):
        return stat_ref[d * STATS + 4 * n : d * STATS + 4 * n + 4, :]

    sum_t, sum_s = stat(0, 0), stat(1, 0)
    for d in range(1, PB):
        sum_t, sum_s = sum_t + stat(0, d), sum_s + stat(1, d)
    norm_t = lax.rsqrt(sum_t / (32 * TD) + EPSILON)
    norm_s = lax.rsqrt(sum_s / (32 * SD) + EPSILON)
    ratio = norm_t / norm_s
    loss = jnp.zeros((4, 128), f32)
    for d in range(PB):
        off = stat(2, d) - ratio
        loss = loss + (stat(3, d) + 2.0 * off * stat(4, d) + (off * stat(0, d)) * off)
    loss_ref[...] = loss * (norm_s * norm_s) * (1.0 / (32 * TD))
    norm_t = jnp.concatenate([norm_t[s : s + 1] for s in range(4)], axis=1)
    norm_s = jnp.concatenate([norm_s[s : s + 1] for s in range(4)], axis=1)
    for h in range(4):
        sl = slice(h * 128, (h + 1) * 128)
        target = jnp.concatenate([ot_ref[s, :, sl] for s in range(4)], axis=1).astype(f32) * norm_t
        feature = jnp.concatenate([os_ref[s, :, sl] for s in range(4)], axis=1).astype(f32) * norm_s
        feature = feature.astype(bf16)
        difference = dot_tn(w_ref[p * 4 + h], feature) - target
        high = difference.astype(bf16)
        low = (difference - high.astype(f32)).astype(bf16)
        grad_ref[h * 64 : (h + 1) * 64, :] = (dot_nt(feature, high) + dot_nt(feature, low)) * (
            1.0 / math.sqrt(TOKENS)
        )


def distill(out_t, out_s, stats, weight):
    return pl.pallas_call(
        distill_kernel,
        out_shape=[jax.ShapeDtypeStruct((256, 128), f32), jax.ShapeDtypeStruct((4, 128), f32)],
        in_specs=[whole()] * 4,
        out_specs=[whole()] * 2,
        compiler_params=params(16),
        name="distill",
    )(out_t, out_s, stats, weight)


def local(teacher_q, teacher_k, teacher_v, student_q, student_k, student_v, doc_ids, proj_weight):
    p, a = lax.axis_index("pb"), lax.axis_index("ha")
    sent = pack(
        pack_kernel, (BLOCK, 384), teacher_k, teacher_v, student_k, student_v, doc_ids.reshape(1, ROWS)
    )
    rounds = [permute(sent[j], to_group(j)) for j in range(4)]
    own = join(rounds)
    up = from_z(own)
    far = from_x(own, 2)
    right, left = from_x(own, 1), from_x(own, -1)
    queries = pack(pack_queries_kernel, (ROWS, 768), teacher_q, student_q)
    swapped = {0: from_core(own)}
    queries, swapped[0] = lax.optimization_barrier((queries, swapped[0]))
    queries = [permute(queries[j], to_group(j)) for j in range(4)]
    parts = [own, right, left, far, up, from_x(up, 1), from_x(up, -1), from_z(far)]
    others = [swapped[u] if u in swapped else from_core(parts[u]) for u in range(8)]
    out_t, out_s, stats = attend(queries, parts, others, proj_weight)
    stats = lax.all_to_all(stats, "pb", split_axis=0, concat_axis=0, tiled=True)
    grad, loss = distill(out_t, out_s, stats, proj_weight)
    other = from_core(loss)
    loss = jnp.where((p // 4 + p) % 2 == a, loss, other)
    loss = lax.dynamic_slice(loss, (p % 4, a * 64), (1, 64)).reshape(64)
    grad = lax.all_to_all(grad, ("kv", "ha"), split_axis=0, concat_axis=0, tiled=True)
    return jnp.sum(grad.reshape(16, 16, 128), axis=0), loss


def solution(mesh):
    in_specs = (
        P(("pb", "kv"), "ha"),
        P(("pb", "kv"), "ha"),
        P(("pb", "kv"), "ha"),
        P(("pb", "kv"), "ha"),
        P(("pb", "kv"), "ha"),
        P(("pb", "kv"), "ha"),
        P(("pb", "kv")),
        P(),
    )
    out_specs = (P(("pb", "kv", "ha"), None), P(("pb", "kv", "ha")))
    return jax.shard_map(local, mesh=mesh, in_specs=in_specs, out_specs=out_specs, check_vma=False)
```

```python
import functools
import math

import jax
import jax.numpy as jnp
from jax import lax
from jax.experimental import pallas as pl
from jax.experimental.pallas import tpu as pltpu
from jax.sharding import PartitionSpec as P

TD = 128
SD = 64
PB, KV, HA = 8, 8, 2
ROWS = 128
PAD = 16
BLOCK = ROWS + PAD
UNIT = 4 * ROWS + PAD
STATS = 24
TOKENS = PB * KV * ROWS
COLS = 512
ALL = ("pb", "kv", "ha")
NEGATIVE = -1e30
EPSILON = 1e-06
LOG2E = 1.4426950408889634
SCALE_T = LOG2E / math.sqrt(TD)
SCALE_S = LOG2E / math.sqrt(SD)
f32 = jnp.float32
bf16 = jnp.bfloat16
VMEM = pltpu.VMEM


def index(pb, kv, ha):
    return (pb * KV + kv) * HA + ha


def core_of(p):
    return (p // 4 + p) % 2


def permute(x, move):
    pairs = [
        (index(p, k, a), index(*move(p, k, a))) for p in range(PB) for k in range(KV) for a in range(HA)
    ]
    return lax.ppermute(x, ALL, pairs)


def from_x(x, step):
    return permute(x, lambda p, k, a: (p, (((k // 2) - step) % 4) * 2 + k % 2, a))


def from_z(x):
    return permute(x, lambda p, k, a: (p, k ^ 1, a))


def from_core(x):
    return permute(x, lambda p, k, a: (p, k, 1 - a))


def to_group(j):
    return lambda p, k, a: (4 * a + (j + p) % 4, k, core_of(p))


def params(mib):
    return pltpu.CompilerParams(vmem_limit_bytes=mib * 1024 * 1024)


def whole(space=None):
    return pl.BlockSpec(memory_space=VMEM if space is None else space)


def bring(pairs, sem):
    copies = [pltpu.make_async_copy(src, dst, sem.at[n]) for n, (src, dst) in enumerate(pairs)]
    for c in copies:
        c.start()
    for c in copies:
        c.wait()


def pack_kernel(tk_, tv_, sk_, sv_, doc_, o0, o1, o2, o3, tk, tv, sk, sv, doc, sem):
    bring([(tk_, tk), (tv_, tv), (sk_, sk), (sv_, sv), (doc_, doc)], sem)
    p = lax.axis_index("pb")
    lane = lax.broadcasted_iota(jnp.int32, (ROWS, 128), 1)
    row = lax.broadcasted_iota(jnp.int32, (PAD, 384), 0)
    ids = doc[...]
    counts = [jnp.sum(jnp.where(ids < d, 1.0, 0.0), axis=1, keepdims=True) for d in (1, 2, 3)]
    for j, out in enumerate((o0, o1, o2, o3)):
        i = lax.rem(p + j, 4)
        odd = lax.rem(i, 2) == 1
        at = pl.ds(pl.multiple_of(i * 128, 128), 128)
        pair = pl.ds(pl.multiple_of((i // 2) * 128, 128), 128)
        out[0:ROWS, 0:128] = tk[:, at]
        out[0:ROWS, 128:256] = tv[:, at].astype(f32).T.astype(bf16)
        keys = sk[:, pair].astype(f32)
        keys = jnp.where(odd, pltpu.roll(keys, 64, 1), keys)
        values = sv[:, pair].astype(f32).T
        values = jnp.where(odd, values[64:128], values[0:64])
        values = jnp.concatenate([pltpu.roll(values, 64, 1), values], axis=0)
        out[0:ROWS, 256:384] = jnp.where(lane < 64, keys, values).astype(bf16)
        pad = jnp.zeros((PAD, 384), f32)
        for d in (1, 2, 3):
            pad = jnp.where(row == 4 * j + d, counts[d - 1], pad)
        out[ROWS:BLOCK, :] = pad.astype(bf16)


def pack_queries_kernel(tq_, sq_, o0, o1, o2, o3, tq, sq, sem):
    bring([(tq_, tq), (sq_, sq)], sem)
    p = lax.axis_index("pb")
    for j, out in enumerate((o0, o1, o2, o3)):
        i = lax.rem(p + j, 4)
        out[:, 0:512] = tq[:, pl.ds(pl.multiple_of(i * 512, 512), 512)]
        out[:, 512:768] = sq[:, pl.ds(pl.multiple_of(i * 256, 256), 256)]


def pack(kernel, shape, *args):
    return pl.pallas_call(
        kernel,
        out_shape=[jax.ShapeDtypeStruct(shape, bf16)] * 4,
        in_specs=[whole(pl.ANY)] * len(args),
        out_specs=[whole()] * 4,
        scratch_shapes=[VMEM(x.shape, x.dtype) for x in args] + [pltpu.SemaphoreType.DMA((len(args),))],
        compiler_params=params(56),
        name="pack",
    )(*args)


def join_kernel(r0, r1, r2, r3, out):
    pad = jnp.zeros((PAD, 384), f32)
    for j, r in enumerate((r0, r1, r2, r3)):
        out[j * ROWS : (j + 1) * ROWS, :] = r[0:ROWS, :]
        pad = pad + r[ROWS:BLOCK, :].astype(f32)
    out[4 * ROWS : UNIT, :] = pad.astype(bf16)


def join(rounds):
    return pl.pallas_call(
        join_kernel,
        out_shape=jax.ShapeDtypeStruct((UNIT, 384), bf16),
        in_specs=[whole()] * 4,
        out_specs=whole(),
        compiler_params=params(8),
        name="join",
    )(*rounds)


def dot_nt(a, b):
    return lax.dot_general(a, b, (((1,), (1,)), ((), ())), preferred_element_type=f32)


def dot_nn(a, b):
    return lax.dot_general(a, b, (((1,), (0,)), ((), ())), preferred_element_type=f32)


def dot_tn(a, b):
    return lax.dot_general(a, b, (((0,), (0,)), ((), ())), preferred_element_type=f32)


def attend_kernel(units, *refs):
    size = len(units)
    tile = 128 * size
    refs = list(refs)

    def take(n):
        out = refs[:n]
        del refs[:n]
        return out

    q_refs = take(4)
    own_parts = take(size)
    other_parts = take(size)
    weight, ot_ref, os_ref, stat_ref = take(4)
    mt, ms, acct, accs, kt, vt, ks, vs, plan, qt, qs, st, ss, pt, ps, at, as_ = refs
    pb, k, b = lax.axis_index("pb"), lax.axis_index("kv"), lax.axis_index("ha")
    i, x, z = pb & 3, k >> 1, k & 1
    chips = []
    for unit in units:
        dx = (0, 1, 3, 2)[unit % 4]
        chips.append(((x + dx) & 3) * 2 + (z if unit < 4 else 1 - z))
    wide = lax.broadcasted_iota(jnp.int32, (ROWS, 128), 1)
    total = jnp.zeros((PAD, 128), f32)
    for side, parts in ((b, own_parts), (1 - b, other_parts)):
        for u, part in enumerate(parts):
            cols = slice(u * 128, (u + 1) * 128)
            for j in range(4):
                rows = slice(j * ROWS, (j + 1) * ROWS)
                g = side * 4 + j
                kt[g, cols, :] = part[rows, 0:128]
                vt[g, 0:TD, cols] = part[rows, 128:256]
                both = part[rows, 256:384]
                ks[g, cols, :] = both
                vs[g, 0:SD, u * 128 : u * 128 + 64] = both[0:64, 64:128]
                vs[g, 0:SD, u * 128 + 64 : (u + 1) * 128] = both[64:128, 64:128]
            total = total + part[4 * ROWS : UNIT, 0:128].astype(f32)
    starts = []
    for d in (1, 2, 3):
        row = total[d : d + 1] + total[d + 4 : d + 5] + total[d + 8 : d + 9] + total[d + 12 : d + 13]
        starts.append(jnp.max(row).astype(jnp.int32))
    for g in range(8):
        vt[g, TD : TD + 16, :] = jnp.ones((16, tile), bf16)
        vs[g, SD : SD + 16, :] = jnp.ones((16, tile), bf16)
    for j in range(4):
        slot = (i - j) & 3
        q = q_refs[j]
        for h in range(4):
            qt[slot, h * 128 : (h + 1) * 128, :] = q[:, h * 128 : (h + 1) * 128]
        for h in range(2):
            two = q[:, 512 + h * 128 : 640 + h * 128].astype(f32)
            qs[slot, h * 256 : h * 256 + 128, :] = jnp.where(wide < 64, two, 0.0).astype(bf16)
            qs[slot, h * 256 + 128 : h * 256 + 256, :] = jnp.where(wide < 64, pltpu.roll(two, 64, 1), 0.0).astype(
                bf16
            )
    for ref in (mt, ms):
        ref[...] = jnp.full((4, 8, COLS), NEGATIVE, f32)
    for ref in (acct, accs):
        ref[...] = jnp.zeros(ref.shape, f32)
    for ref in (at, as_):
        ref[1] = jnp.ones((8, COLS), f32)
    for ref in (pt, ps):
        ref[1] = jnp.zeros((tile, COLS), bf16)

    def doc_start(pos):
        at_ = jnp.where(pos >= starts[0], starts[0], 0)
        at_ = jnp.where(pos >= starts[1], starts[1], at_)
        return jnp.where(pos >= starts[2], starts[2], at_)

    count = jnp.int32(0)
    for slot in range(4):
        p = jnp.where(slot % 2 == b, slot, slot + 4)
        first = p * 1024 + k * 128

        def enter(t, count, slot=slot, first=first):
            plan[0, count + 1] = jnp.int32(slot)
            plan[1, count + 1] = t
            plan[2, count + 1] = (((t >> 2) + t) & 1) * 4 + ((i - t) & 3)
            plan[3, count + 1] = first
            return count + 1

        count = lax.fori_loop(doc_start(first) >> 10, p + 1, enter, count)
    for n in (0, 2):
        plan[n, 0] = plan[n, 1]
        plan[n, count + 1] = plan[n, count]

    def softmax(s_ref, p_ref, m_ref, a_ref, scale):
        old = m_ref[...]
        top = None
        for r in range(0, tile, 64):
            s = jnp.max(s_ref[r : r + 64, :].reshape(8, 8, COLS), axis=0)
            top = s if top is None else jnp.maximum(top, s)
        new = jnp.maximum(old, jnp.max(top, axis=0, keepdims=True))
        for r in range(0, tile, 64):
            w = jnp.exp2((s_ref[r : r + 64, :].reshape(8, 8, COLS) - new[None]) * scale)
            p_ref[r : r + 64, :] = w.reshape(64, COLS).astype(bf16)
        a_ref[...] = jnp.exp2((old - new) * scale)
        m_ref[...] = new

    def rescale(acc, a):
        n = acc.shape[0] // 8
        return (acc.reshape(n, 8, COLS) * a[None]).reshape(n * 8, COLS)

    def mask(n, c):
        slot, tile_at, first = plan[0, n], plan[1, n] * 1024, plan[3, n]
        ds_first, ds_last = doc_start(first), doc_start(first + 127)
        newest = tile_at + 1023 > first

        @pl.when(newest & (ds_last > first))
        def _():
            column = first + (lax.broadcasted_iota(jnp.int32, (8, COLS), 1) & 127)
            for ref in (mt, ms):
                ref[slot] = jnp.where(doc_start(column) > first, NEGATIVE, ref[slot])

        @pl.when((tile_at < ds_first) | newest)
        def _():
            oldest = jnp.where(newest, ds_last, ds_first)
            for u in range(size):
                rows = slice(u * 128, (u + 1) * 128)
                at_ = tile_at + chips[u] * 128
                outside = (at_ + 127 < ds_first) | (at_ > first + 127)

                @pl.when(outside)
                def _(rows=rows):
                    for ref in (st, ss):
                        ref[c, rows, :] = jnp.full((128, COLS), NEGATIVE, f32)

                @pl.when(jnp.logical_not(outside) & ((at_ < oldest) | (at_ + 127 > first)))
                def _(rows=rows, at_=at_):
                    qpos = first + lax.broadcasted_iota(jnp.int32, (128, 128), 1)
                    kpos = at_ + lax.broadcasted_iota(jnp.int32, (128, 128), 0)
                    ok = (kpos <= qpos) & (kpos >= doc_start(qpos))
                    for ref in (st, ss):
                        for h in range(4):
                            sl = slice(h * 128, (h + 1) * 128)
                            ref[c, rows, sl] = jnp.where(ok, ref[c, rows, sl], NEGATIVE)

    def queries_by_keys(n, c):
        slot, g = plan[0, n], plan[2, n]
        st[c] = dot_nt(kt[g], qt[slot])
        ss[c] = dot_nt(ks[g], qs[slot])

    def add_values(n, c):
        slot, g = plan[0, n], plan[2, n]
        acct[slot] = rescale(acct[slot], at[c]) + dot_nn(vt[g], pt[c])
        accs[slot] = rescale(accs[slot], as_[c]) + dot_nn(vs[g], ps[c])

    def half(n, c):
        mask(n, c)
        slot, after, g = plan[0, n], plan[0, n + 1], plan[2, n + 1]
        st[1 - c] = dot_nt(kt[g], qt[after])
        softmax(st.at[c], pt.at[c], mt.at[slot], at.at[c], SCALE_T)
        ss[1 - c] = dot_nt(ks[g], qs[after])
        softmax(ss.at[c], ps.at[c], ms.at[slot], as_.at[c], SCALE_S)
        add_values(n - 1, 1 - c)

    queries_by_keys(1, 0)

    def step(n, c):
        half(2 * n + 1, 0)
        half(2 * n + 2, 1)
        return c

    lax.fori_loop(0, count >> 1, step, 0)
    odd = (count & 1) == 1

    @pl.when(odd)
    def _():
        half(count, 0)
        add_values(count, 0)

    @pl.when(jnp.logical_not(odd))
    def _():
        add_values(count, 1)

    base = pb * 4
    for slot in range(4):
        out_t = (acct[slot, 0:TD, :] / acct[slot, TD : TD + 1, :]).astype(bf16)
        out_s = (accs[slot, 0:SD, :] / accs[slot, SD : SD + 1, :]).astype(bf16)
        ot_ref[slot] = out_t
        os_ref[slot] = out_s
        targets = [out_t[:, h * 128 : (h + 1) * 128].astype(f32) for h in range(4)]
        students = [out_s[:, h * 128 : (h + 1) * 128] for h in range(4)]
        predicted = [dot_tn(weight[base + h], students[h]) for h in range(4)]

        def across(pieces):
            total = pieces[0]
            for piece in pieces[1:]:
                total = total + piece
            return jnp.sum(total, axis=0, keepdims=True)

        sum_t = across([t * t for t in targets])
        sum_s = across([s.astype(f32) * s.astype(f32) for s in students])
        cross = across([y * t for y, t in zip(predicted, targets)])
        kappa = jnp.where(sum_t > 0.0, cross / jnp.where(sum_t > 0.0, sum_t, 1.0), 0.0)
        rest = [y - kappa * t for y, t in zip(predicted, targets)]
        sum_e = across([y * y for y in rest])
        sum_x = across([y * t for y, t in zip(rest, targets)])
        for n, value in enumerate((sum_t, sum_s, kappa, sum_e, sum_x)):
            for d in range(PB):
                stat_ref[d * STATS + n * 4 + slot : d * STATS + n * 4 + slot + 1, :] = value
    for d in range(PB):
        stat_ref[d * STATS + 20 : (d + 1) * STATS, :] = jnp.zeros((STATS - 20, 128), f32)


def attend(queries, own_parts, other_parts, weight):
    size = len(own_parts)
    tile = 128 * size
    args = [*queries, *own_parts, *other_parts, weight]
    return pl.pallas_call(
        functools.partial(attend_kernel, tuple(range(size))),
        out_shape=[
            jax.ShapeDtypeStruct((4, TD, COLS), bf16),
            jax.ShapeDtypeStruct((4, SD, COLS), bf16),
            jax.ShapeDtypeStruct((PB * STATS, 128), f32),
        ],
        in_specs=[whole()] * len(args),
        out_specs=[whole()] * 3,
        scratch_shapes=[VMEM((4, 8, COLS), f32)] * 2
        + [
            VMEM((4, TD + 16, COLS), f32),
            VMEM((4, SD + 16, COLS), f32),
            VMEM((8, tile, 128), bf16),
            VMEM((8, TD + 16, tile), bf16),
            VMEM((8, tile, 128), bf16),
            VMEM((8, SD + 16, tile), bf16),
            pltpu.SMEM((4, 40), jnp.int32),
        ]
        + [VMEM((4, COLS, 128), bf16)] * 2
        + [VMEM((2, tile, COLS), f32)] * 2
        + [VMEM((2, tile, COLS), bf16)] * 2
        + [VMEM((2, 8, COLS), f32)] * 2,
        compiler_params=params(40),
        name="attend",
    )(*args)


def distill_kernel(ot_ref, os_ref, stat_ref, w_ref, grad_ref, loss_ref):
    p, b = lax.axis_index("pb"), lax.axis_index("ha")

    def stat(n, d):
        return stat_ref[d * STATS + 4 * n : d * STATS + 4 * n + 4, :]

    sum_t, sum_s = stat(0, 0), stat(1, 0)
    for d in range(1, PB):
        sum_t, sum_s = sum_t + stat(0, d), sum_s + stat(1, d)
    norm_t = lax.rsqrt(sum_t / (32 * TD) + EPSILON)
    norm_s = lax.rsqrt(sum_s / (32 * SD) + EPSILON)
    ratio = norm_t / norm_s
    loss = jnp.zeros((4, 128), f32)
    for d in range(PB):
        off = stat(2, d) - ratio
        loss = loss + (stat(3, d) + 2.0 * off * stat(4, d) + (off * stat(0, d)) * off)
    loss_ref[...] = loss * (norm_s * norm_s) * (1.0 / (32 * TD))
    norm_t = jnp.concatenate([norm_t[s : s + 1] for s in range(4)], axis=1)
    norm_s = jnp.concatenate([norm_s[s : s + 1] for s in range(4)], axis=1)
    for h in range(4):
        sl = slice(h * 128, (h + 1) * 128)
        target = jnp.concatenate([ot_ref[s, :, sl] for s in range(4)], axis=1).astype(f32) * norm_t
        feature = jnp.concatenate([os_ref[s, :, sl] for s in range(4)], axis=1).astype(f32) * norm_s
        feature = feature.astype(bf16)
        difference = dot_tn(w_ref[p * 4 + h], feature) - target
        high = difference.astype(bf16)
        low = (difference - high.astype(f32)).astype(bf16)
        grad_ref[h * 64 : (h + 1) * 64, :] = (dot_nt(feature, high) + dot_nt(feature, low)) * (
            1.0 / math.sqrt(TOKENS)
        )


def distill(out_t, out_s, stats, weight):
    return pl.pallas_call(
        distill_kernel,
        out_shape=[jax.ShapeDtypeStruct((256, 128), f32), jax.ShapeDtypeStruct((4, 128), f32)],
        in_specs=[whole()] * 4,
        out_specs=[whole()] * 2,
        compiler_params=params(16),
        name="distill",
    )(out_t, out_s, stats, weight)


def local(teacher_q, teacher_k, teacher_v, student_q, student_k, student_v, doc_ids, proj_weight):
    p, a = lax.axis_index("pb"), lax.axis_index("ha")
    sent = pack(
        pack_kernel, (BLOCK, 384), teacher_k, teacher_v, student_k, student_v, doc_ids.reshape(1, ROWS)
    )
    rounds = [permute(sent[j], to_group(j)) for j in range(4)]
    own = join(rounds)
    up = from_z(own)
    far = from_x(own, 2)
    right, left = from_x(own, 1), from_x(own, -1)
    queries = pack(pack_queries_kernel, (ROWS, 768), teacher_q, student_q)
    swapped = {0: from_core(own)}
    queries, swapped[0] = lax.optimization_barrier((queries, swapped[0]))
    queries = [permute(queries[j], to_group(j)) for j in range(4)]
    parts = [own, right, left, far, up, from_x(up, 1), from_x(up, -1), from_z(far)]
    others = [swapped[u] if u in swapped else from_core(parts[u]) for u in range(8)]
    out_t, out_s, stats = attend(queries, parts, others, proj_weight)
    stats = lax.all_to_all(stats, "pb", split_axis=0, concat_axis=0, tiled=True)
    grad, loss = distill(out_t, out_s, stats, proj_weight)
    other = from_core(loss)
    loss = jnp.where((p // 4 + p) % 2 == a, loss, other)
    loss = lax.dynamic_slice(loss, (p % 4, a * 64), (1, 64)).reshape(64)
    grad = lax.all_to_all(grad, ("kv", "ha"), split_axis=0, concat_axis=0, tiled=True)
    return jnp.sum(grad.reshape(16, 16, 128), axis=0), loss


def solution(mesh):
    in_specs = (
        P(("pb", "kv"), "ha"),
        P(("pb", "kv"), "ha"),
        P(("pb", "kv"), "ha"),
        P(("pb", "kv"), "ha"),
        P(("pb", "kv"), "ha"),
        P(("pb", "kv"), "ha"),
        P(("pb", "kv")),
        P(),
    )
    out_specs = (P(("pb", "kv", "ha"), None), P(("pb", "kv", "ha")))
    return jax.shard_map(local, mesh=mesh, in_specs=in_specs, out_specs=out_specs, check_vma=False)
```
